128 devices in a mesh: dp: 8 (over z, core), mp: 16 (over x, y).
Axes of the slice: x: 4, y: 4, z: 4, core: 2. Of those that a mesh axis runs over, the one named last changes fastest.
Arguments:
- grad_query: bfloat16 [2, 64, 294912], P(None, None, ('dp', 'mp')), may hold values from -100 to 100
- grad_key: bfloat16 [2, 64, 65536], P(None, None, ('dp', 'mp')), may hold values from -100 to 100
- weight_query: bfloat16 [2, 64, 294912], P(None, None, ('dp', 'mp')), may hold values from -6 to 6
- weight_key: bfloat16 [2, 64, 65536], P(None, None, ('dp', 'mp')), may hold values from -6 to 6
- moment_query: float32 [256, 294912], P(('dp', 'mp')), may hold values from -6 to 6
- moment_key: float32 [256, 65536], P(('dp', 'mp')), may hold values from -6 to 6
- logit_peak: bfloat16 [8, 2, 64], P('dp'), may hold values from 5 to 400
- owner_table: int32 [64, 2, 1], replicated, may hold values from 0 to 7; in each aligned block of 8 rows (0 to 7, 8 to 15, ..., all dimensions but the last counted through in order) at most 2 rows name the same one
- head_order: int32 [64], replicated, may hold values from 0 to 63, each once
Outputs:
- query_rollout: bfloat16 [2, 64, 294912], P(None, 'mp', 'dp')
- key_rollout: bfloat16 [2, 64, 65536], P(None, 'mp', 'dp')
- query_moment_out: float32 [256, 294912], P(('dp', 'mp'))
- key_moment_out: float32 [256, 65536], P(('dp', 'mp'))
The draws below stay inside these ranges and needn't reach their ends.
Inputs may be any that keep to these rules, and one draw needn't show every extreme that they name: `owner_table`: among the 8 rows of one rollout rank (positions r * 4 to (r + 1) * 4 - 1, all layers), no dp index is named by more than 2 rows. `head_order`: A permutation of the heads.
All inputs are finite; a program needn't handle non-finite values.
Results may differ from the reference program's by a relative error of at most 0.0045.
Values may be sent and summed in bfloat16 or wider, within the bound.
No kernel may reach another device: no remote copies, remote signals or barrier semaphores. Data moves between devices by JAX's collectives and lax.ppermute only.
A program may use at most 64 MiB of HBM per device.

```python
import math
import jax
import jax.numpy as jnp
import numpy as np
from jax import lax

H = 64
DN = 128
RQ = 1536
RK = 512
LAYERS = 2
ITERS = 5
DQ = 192
UPR = 8
MOST = 2
N_DP = 8
N_MP = 16


def scale_profile(key, shape, low, high):
    return jnp.exp(jax.random.uniform(key, shape, jnp.float32, math.log(low), math.log(high)))


def rough_gradient(key, row_count, column_count, salt):
    key = jax.random.fold_in(key, salt)
    noise_key, row_key, column_key = jax.random.split(key, 3)
    shape = (LAYERS, H, row_count, column_count)
    noise = jnp.clip(jax.random.normal(noise_key, shape, jnp.float32), -6.0, 6.0)
    low, high = (0.3, 3.0)
    row_scale = scale_profile(row_key, (LAYERS, H, row_count, 1), low, high)
    column_scale = scale_profile(column_key, (LAYERS, H, 1, column_count), low, high)
    return (noise * row_scale * column_scale).reshape(LAYERS, H, row_count * column_count)


def draw_grad_query(key, part):
    return rough_gradient(key, DQ, RQ, 11).astype(jnp.bfloat16)


def draw_grad_key(key, part):
    return rough_gradient(key, DN, RK, 17).astype(jnp.bfloat16)


def draw_logit_peak(key, part):
    key = jax.random.fold_in(key, 29)
    base_key, rough_key = jax.random.split(key)
    low, rough_low = (30.0, 0.75)
    base = scale_profile(base_key, (1, LAYERS, H), low, 400.0)
    ramp = ((1.0 + 2.0 * jnp.arange(N_DP, dtype=jnp.float32) / (N_DP - 1)) / 3.0)[:, None, None]
    rough = jax.random.uniform(rough_key, (N_DP, LAYERS, H), jnp.float32, rough_low, 1.0)
    return (base * ramp * rough).astype(jnp.bfloat16)


def block_scale(rng, shape, shards, least, largest):
    def one(dim, blocks):
        draws = jax.random.uniform(jax.random.fold_in(jax.random.fold_in(rng, 6), dim), (blocks,), jnp.float32, least / len(shards), largest / len(shards))
        return jnp.repeat(jnp.exp(draws), shape[dim] // blocks).reshape((-1,) + (1,) * (len(shape) - dim - 1))

    factor_of = one(*shards[0])
    for cut in shards[1:]:
        factor_of = factor_of * one(*cut)
    return factor_of


def deal_out(own_key, own, number, rows, number_of, top, most, lean):
    order = jax.random.permutation(own_key, number_of)
    packed, usual = shares(number_of, rows * top, most, lean, True), shares(number_of, rows * top, most, lean, False)
    places = jnp.arange(number_of)

    def named(lengths, turn):
        used = int((lengths > 0).sum())
        fixed = max(1, used // 4)
        shifted = fixed + (places - fixed + turn * (used - fixed)) % max(1, number_of - fixed)
        return jnp.zeros((number_of,), jnp.int32).at[order[jnp.where(places < fixed, places, shifted)]].set(jnp.asarray(lengths, jnp.int32))

    lengths = jnp.where(number % 4 == 0, named(packed, number // 4), named(usual, number - number // 4 - 1))
    mixed = jax.random.permutation(jax.random.fold_in(own, 3), number_of)
    giver, taker = mixed[0:number_of // 2 * 2:2], mixed[1:number_of // 2 * 2:2]
    room = jnp.minimum(lengths[giver] - 1, most - lengths[taker]) // 2
    room = jnp.where((giver == order[0]) | (taker == order[0]) | (lengths[taker] == 0), 0, jnp.maximum(room, 0))
    shifted = jax.random.randint(jax.random.fold_in(own, 4), (number_of // 2,), 0, 1 << 20) % (room + 1)
    lengths = lengths.at[giver].add(-shifted).at[taker].add(shifted)
    items = jnp.searchsorted(jnp.cumsum(lengths), jnp.arange(rows * top), side="right").astype(jnp.int32)
    listing = items.reshape(top, rows).T
    listing = listing[jax.random.permutation(jax.random.fold_in(own, 1), rows)]
    turn = jax.random.randint(jax.random.fold_in(own, 2), (rows, 1), 0, top)
    return jnp.take_along_axis(listing, (jnp.arange(top)[None, :] + turn) % top, axis=1)


def shares(count, total, limit, skew, full):
    weights = [(1 << 20) // math.isqrt(standing ** skew) + 1 for standing in range(1, count + 1)]
    largest = limit if full else min(limit, max(-(-total // count), total * weights[0] // sum(weights)))
    least = 1 if total - largest >= count - 1 else 0
    holding, rest = [largest] + [least] * (count - 1), total - largest - least * (count - 1)
    while rest > 0:
        free = [i for i in range(1, count) if holding[i] < largest] or [i for i in range(1, count) if holding[i] < limit]
        pool, budget = sum([weights[i] for i in free]), rest
        for i in free:
            more = min(limit - holding[i], max(1, budget * weights[i] // pool), rest)
            holding[i] = holding[i] + more
            rest = rest - more
    return np.array(holding)


def centred(key, extent, spread, reach, cuts=(), held_as=jnp.bfloat16):
    factor_of = block_scale(key, extent, cuts, -0.22, 0.18) if cuts else 1.0
    entries = jax.random.normal(key, extent, jnp.float32) * spread * factor_of
    return jnp.minimum(jnp.maximum(entries, -reach), reach).astype(held_as)


def setup_inputs(seed: int = 0) -> dict:
    arg_keys = jax.random.split(jax.random.key(seed), 10)
    grad_query = draw_grad_query(jax.random.fold_in(arg_keys[9], 71), 0)
    grad_key = draw_grad_key(jax.random.fold_in(arg_keys[9], 71), 0)
    weight_query = centred(arg_keys[2], (LAYERS, H, DQ * RQ), 1.0, 6.0, ((2, 128),))
    weight_key = centred(arg_keys[3], (LAYERS, H, DN * RK), 1.0, 6.0, ((2, 128),))
    moment_query = centred(arg_keys[4], (N_DP * N_MP * MOST, DQ * RQ), 1.0, 6.0, ((0, 128),), jnp.float32)
    moment_key = centred(arg_keys[5], (N_DP * N_MP * MOST, DN * RK), 1.0, 6.0, ((0, 128),), jnp.float32)
    logit_peak = draw_logit_peak(jax.random.fold_in(arg_keys[9], 71), 0)
    owner_table_keys = jax.random.split(jax.random.fold_in(arg_keys[7], 1), H * LAYERS // UPR)
    owner_table_turns = jax.random.permutation(jax.random.fold_in(arg_keys[7], 3), H * LAYERS // UPR)
    owner_table = jax.vmap(lambda own, number: deal_out(jax.random.fold_in(arg_keys[7], 2), own, number, UPR, N_DP, 1, MOST, 2))(owner_table_keys, owner_table_turns).reshape((H, LAYERS, 1))
    head_order = jax.random.permutation(arg_keys[8], H).astype(jnp.int32)
    return {"grad_query": grad_query, "grad_key": grad_key, "weight_query": weight_query, "weight_key": weight_key, "moment_query": moment_query, "moment_key": moment_key, "logit_peak": logit_peak, "owner_table": owner_table, "head_order": head_order}


quintic_one = 3.4445
quintic_two = -4.775
quintic_three = 2.0315
momentum_decay = 0.95
step_size = 0.5
logit_cap = 100.0

def owner_slots(owners, rank_count, capacity, owner_count):
    head_count, layer_count = owners.shape
    per_rank = head_count // rank_count
    blocks = owners.reshape(rank_count, per_rank * layer_count)
    matches = (blocks[:, :, None] == jnp.arange(owner_count, dtype=jnp.int32)[None, None, :]).astype(jnp.int32)
    earlier = (jnp.cumsum(matches, axis=1) - matches).astype(jnp.int32)
    slot_number = lax.optimization_barrier(jnp.sum(earlier * matches, axis=2)).astype(jnp.int32)
    rank_number = jnp.arange(rank_count, dtype=jnp.int32)[:, None]
    device_number = blocks * rank_count + rank_number
    return (device_number * capacity + slot_number).astype(jnp.int32).reshape(head_count, layer_count)

def orthogonalize(moment):
    scaled = (moment / (jnp.sqrt(jnp.sum(moment * moment)) + 1e-07)).astype(jnp.bfloat16)
    for sweep_index in range(ITERS):
        gram_matrix = jnp.dot(scaled, scaled.T, preferred_element_type=jnp.float32).astype(jnp.bfloat16)
        square = jnp.dot(gram_matrix, gram_matrix, preferred_element_type=jnp.float32)
        mixing = (quintic_two * gram_matrix.astype(jnp.float32) + quintic_three * square).astype(jnp.bfloat16)
        scaled = (quintic_one * scaled.astype(jnp.float32) + jnp.dot(mixing, scaled, preferred_element_type=jnp.float32)).astype(jnp.bfloat16)
    return scaled

def refresh(moment, gradient, weight, factor, row_count, column_count, nope_rows):
    moment_next = momentum_decay * moment + gradient.astype(jnp.float32)
    polar_factor = orthogonalize(moment_next.reshape(row_count, column_count))
    stepped = weight.astype(jnp.float32).reshape(row_count, column_count) - step_size * 0.2 * math.sqrt(max(row_count, column_count)) * polar_factor.astype(jnp.float32)
    row_index = jnp.arange(row_count, dtype=jnp.int32)
    row_factor = jnp.where(row_index < nope_rows, jnp.sqrt(factor), factor)
    return (moment_next, (stepped * row_factor[:, None]).astype(jnp.bfloat16).reshape(-1))

def reference(grad_query, grad_key, weight_query, weight_key, moment_query, moment_key, logit_peak, owner_table, head_order):
    target = owner_slots(owner_table[:, :, 0], N_MP, MOST, N_DP)
    peak_table = lax.optimization_barrier(jnp.max(logit_peak.astype(jnp.float32), axis=0))
    clip_table = jnp.minimum(1.0, logit_cap / peak_table)
    slot_list = target.T.reshape(-1)
    layer_list = jnp.repeat(jnp.arange(LAYERS, dtype=jnp.int32), H)
    head_list = jnp.tile(head_order, LAYERS)

    def one_unit(unit_index):
        slot = slot_list[unit_index]
        layer = layer_list[unit_index]
        head = head_list[unit_index]
        factor = clip_table[layer, head]
        query_next, query_block = refresh(moment_query[slot], grad_query[layer, head], weight_query[layer, head], factor, DQ, RQ, DN)
        key_next, key_block = refresh(moment_key[slot], grad_key[layer, head], weight_key[layer, head], factor, DN, RK, DN)
        return (query_next, key_next, query_block, key_block)
    query_moments, key_moments, query_blocks, key_blocks = lax.map(one_unit, jnp.arange(LAYERS * H, dtype=jnp.int32))
    query_moment_out = moment_query.at[slot_list].set(query_moments)
    key_moment_out = moment_key.at[slot_list].set(key_moments)
    return (query_blocks.reshape(LAYERS, H, DQ * RQ), key_blocks.reshape(LAYERS, H, DN * RK), query_moment_out, key_moment_out)
```

```python
import functools
import math

import jax
import jax.numpy as jnp
from jax import lax
from jax.experimental import pallas as pl
from jax.experimental.pallas import tpu as pltpu
from jax.sharding import PartitionSpec as P

DN = 128
RQ = 1536
RK = 512
ITERS = 5
DQ = 192
LANE = 128

quintic_one = 3.4445
quintic_two = -4.775
quintic_three = 2.0315
momentum_decay = 0.95
step_size = 0.5
logit_cap = 100.0

f32 = jnp.float32
bf16 = jnp.bfloat16
VMEM = pl.BlockSpec(memory_space=pltpu.VMEM)
SMEM = pl.BlockSpec(memory_space=pltpu.SMEM)


def iota(shape, dim):
    return lax.broadcasted_iota(jnp.int32, shape, dim)


def dot(a, b, dims=((1,), (0,))):
    return lax.dot_general(a, b, (dims, ((), ())), preferred_element_type=f32)


def head_matrix(head_ref, heads):
    return (iota((heads, heads), 0) == head_ref[...]).astype(bf16)


def pack_grads_kernel(owner_ref, head_ref, gq_ref, gk_ref, out_ref, stage, *, ranks, owners, slots):
    heads, layers = owner_ref.shape
    devices = ranks * owners
    per_rank = heads // ranks
    tq = gq_ref.shape[1] // LANE
    tk = gk_ref.shape[1] // LANE
    rows = (tq + tk) * slots
    by_row = owner_ref[...].astype(f32)
    eye = (iota((heads, heads), 0) == iota((heads, heads), 1)).astype(f32)
    by_lane = dot(by_row, eye, ((0,), (0,)))
    other, mine = iota((heads, heads), 0), iota((heads, heads), 1)
    same_rank = (other // per_rank) == (mine // per_rank)
    heads_of = head_matrix(head_ref, heads)
    lane_rank = iota((1, heads), 1) // per_rank
    picks = [[None] * layers for _ in range(slots)]
    for layer in range(layers):
        owner = by_lane[layer : layer + 1, :]
        earlier = jnp.zeros((1, heads), f32)
        for before in range(layers):
            ahead = (other <= mine) if before < layer else (other < mine)
            hit = same_rank & ahead & (by_row[:, before : before + 1] == owner)
            earlier += jnp.sum(hit.astype(f32), axis=0, keepdims=True)
        target = (owner.astype(jnp.int32) * ranks + lane_rank) * slots + earlier.astype(jnp.int32)
        for slot in range(slots):
            chosen = (iota((devices, heads), 0) * slots + slot == target).astype(bf16)
            picks[slot][layer] = dot(chosen, heads_of, ((1,), (1,))).astype(bf16)
    for slot in range(slots):
        pick = jnp.concatenate(picks[slot], axis=1)
        for ref, tiles, base in ((gq_ref, tq, 0), (gk_ref, tk, tq)):
            value = dot(pick, ref[...])
            for tile in range(tiles):
                stage[pl.ds((base + tile) * slots + slot, devices, stride=rows), :] = value[
                    :, tile * LANE : (tile + 1) * LANE
                ]
    out_ref[...] = stage[...].astype(bf16)


def pack_weights_kernel(head_ref, wq_ref, wk_ref, out_ref, stage, *, ranks):
    layers, heads, _ = wq_ref.shape
    per_rank = heads // ranks
    tq = wq_ref.shape[2] // LANE
    tk = wk_ref.shape[2] // LANE
    rows = layers * (tq + tk) * per_rank
    heads_of = head_matrix(head_ref, heads)
    place, position = iota((heads, heads), 0), iota((heads, heads), 1)
    order = (position == (place % ranks) * per_rank + place // ranks).astype(bf16)
    pick = dot(order, heads_of, ((1,), (1,))).astype(bf16)
    for layer in range(layers):
        for ref, tiles, base in ((wq_ref, tq, 0), (wk_ref, tk, tq)):
            value = dot(pick, ref[layer])
            for tile in range(tiles):
                first = (layer * (tq + tk) + base + tile) * per_rank
                for place_in in range(per_rank):
                    stage[pl.ds(first + place_in, ranks, stride=rows), :] = value[
                        place_in * ranks : (place_in + 1) * ranks, tile * LANE : (tile + 1) * LANE
                    ]
    out_ref[...] = stage[...].astype(bf16)


def polar_kernel(
    owner_ref, recv_ref, mq_ref, mk_ref, peak_ref, out_ref, mq_out, mk_out, flat_q, flat_k, *, ranks, owners, slots
):
    here_owner = lax.axis_index("dp")
    here_rank = lax.axis_index("mp")
    devices = ranks * owners
    unit_rows = owner_ref.shape[0] // ranks
    held = jnp.int32(0)
    for unit in range(unit_rows):
        held += (owner_ref[here_rank * unit_rows + unit] == here_owner).astype(jnp.int32)
    sub = iota((8, LANE), 0)
    filled = (sub % slots) < held
    low = sub < 4
    tq = DQ * RQ // LANE // devices * slots
    tk = DN * RK // LANE // devices * slots
    rows = tq + tk

    def tile_of(value, index):
        return value[index * 8 : (index + 1) * 8, :]

    def step(quad, carry):
        block = recv_ref[pl.ds(pl.multiple_of(quad * 4 * rows, 16), 4 * rows), :].astype(f32)
        for pair in range(2):
            g = [tile_of(block, pair * 11 + j) for j in range(11)]
            query = g[0:4] + [jnp.where(low, g[4], g[5])] + g[6:10]
            key = [pltpu.roll(jnp.where(low, g[5], g[4]), 4, 0), g[10]]
            for grads, ref, out, count in ((query, mq_ref, mq_out, 9), (key, mk_ref, mk_out, 2)):
                base = pl.multiple_of((quad * 2 + pair) * count * 8, 8)
                for j in range(count):
                    at = pl.ds(pl.multiple_of(base + j * 8, 8), 8)
                    old = ref[at, :]
                    out[at, :] = jnp.where(filled, momentum_decay * old + grads[j], old)
        return carry

    lax.fori_loop(0, devices // 4, step, 0)

    chains = []
    for slot in range(slots):
        for ref, height, width in ((mq_out, DQ, RQ), (mk_out, DN, RK)):
            tiles = width // LANE
            parts = [ref[pl.ds(tile * slots + slot, height, stride=tiles * slots), :] for tile in range(tiles)]
            total = jnp.zeros((height, LANE), f32)
            for part in parts:
                total += part * part
            norm = jnp.sqrt(jnp.sum(total, keepdims=True))
            scale = 1.0 / (norm + 1e-07)
            chains.append(jnp.concatenate([(part * scale).astype(bf16) for part in parts], axis=1))
    for _ in range(ITERS):
        grams = [dot(x, x, ((1,), (1,))).astype(bf16) for x in chains]
        squares = [dot(a, a) for a in grams]
        mixings = [
            (quintic_two * a.astype(f32) + quintic_three * s).astype(bf16) for a, s in zip(grams, squares)
        ]
        products = [dot(b, x) for b, x in zip(mixings, chains)]
        chains = [(quintic_one * x.astype(f32) + y).astype(bf16) for x, y in zip(chains, products)]
    fq = DQ * RQ // LANE // owners
    fk = DN * RK // LANE // owners
    for slot in range(slots):
        for x, flat, height, width in (
            (chains[slot * 2], flat_q, DQ, RQ),
            (chains[slot * 2 + 1], flat_k, DN, RK),
        ):
            tiles = width // LANE
            for tile in range(tiles):
                flat[pl.ds(tile, height, stride=tiles), :] = x[:, tile * LANE : (tile + 1) * LANE].astype(f32)
        for owner in range(owners):
            at = slot * (fq + fk)
            out_ref[owner, at : at + fq, :] = flat_q[owner * fq : (owner + 1) * fq, :].astype(bf16)
            out_ref[owner, at + fq : at + fq + fk, :] = flat_k[owner * fk : (owner + 1) * fk, :].astype(bf16)
    peaks = jnp.concatenate([peak_ref[...].astype(f32), jnp.zeros((14, 64), f32)], axis=0)
    peaks = jnp.concatenate([peaks, jnp.zeros((16, 64), f32)], axis=1).astype(bf16)
    for owner in range(owners):
        out_ref[owner, slots * (fq + fk) :, :] = peaks


def finish_kernel(owner_ref, head_ref, polar_ref, weight_ref, q_out, k_out, spread_q, spread_k, *, ranks, owners, slots):
    here_owner = lax.axis_index("dp")
    here_rank = lax.axis_index("mp")
    heads = head_ref.shape[0]
    unit_rows = owner_ref.shape[0] // ranks
    per_rank = heads // ranks
    layers = unit_rows // per_rank
    fq = DQ * RQ // LANE // owners
    fk = DN * RK // LANE // owners
    peaks = polar_ref[0, slots * (fq + fk) :, :].astype(f32)
    for owner in range(1, owners):
        peaks = jnp.maximum(peaks, polar_ref[owner, slots * (fq + fk) :, :].astype(f32))
    names = [owner_ref[here_rank * unit_rows + unit] for unit in range(unit_rows)]
    sub, lane = iota((8, LANE), 0), iota((8, LANE), 1)
    head_of = jnp.zeros((8, LANE), jnp.int32)
    for place in range(per_rank):
        head_of = jnp.where(sub % per_rank == place, head_ref[here_rank * per_rank + place], head_of)
    row_height = RQ // LANE
    for layer in range(layers):
        peak = jnp.sum(
            jnp.where(head_of == lane, jnp.broadcast_to(peaks[layer : layer + 1, :], (8, LANE)), 0.0),
            axis=1,
            keepdims=True,
        )
        factor = jnp.broadcast_to(jnp.minimum(1.0, logit_cap / peak), (8, LANE))
        root = jnp.sqrt(factor)
        for place in range(per_rank):
            unit = place * layers + layer
            earlier = jnp.int32(0)
            for before in range(unit):
                earlier += (names[before] == names[unit]).astype(jnp.int32)
            start = pl.multiple_of(earlier * (fq + fk), 16)
            block = polar_ref[names[unit], pl.ds(start, fq + fk), :].astype(f32)
            spread_q[pl.ds(layer * fq * per_rank + place, fq, stride=per_rank), :] = block[:fq]
            spread_k[pl.ds(layer * fk * per_rank + place, fk, stride=per_rank), :] = block[fq:]
        sq = fq // ranks * per_rank
        sk = fk // ranks * per_rank
        cq = step_size * 0.2 * math.sqrt(max(DQ, RQ))
        ck = step_size * 0.2 * math.sqrt(max(DN, RK))
        span = sq + sk
        for pair in range(ranks // 2):
            held = [
                weight_ref[2 * pair + j].astype(f32)[layer * span : (layer + 1) * span] for j in range(2)
            ]
            wq = jnp.concatenate([x[:sq] for x in held], axis=0)
            wk = jnp.concatenate([x[sq:] for x in held], axis=0)
            at = layer * fq * per_rank + pair * 2 * sq
            stepped = wq - cq * spread_q[at : at + 2 * sq, :]
            tiles = []
            for tile in range(2 * sq // 8):
                row = here_owner * (DQ // owners) + (pair * 2 * sq + tile * 8) // per_rank // row_height
                tiles.append(stepped[tile * 8 : tile * 8 + 8] * jnp.where(row < DN, root, factor))
            q_out[at : at + 2 * sq, :] = jnp.concatenate(tiles, axis=0).astype(bf16)
            at = layer * fk * per_rank + pair * 2 * sk
            stepped = wk - ck * spread_k[at : at + 2 * sk, :]
            tiles = [stepped[tile * 8 : tile * 8 + 8] * root for tile in range(2 * sk // 8)]
            k_out[at : at + 2 * sk, :] = jnp.concatenate(tiles, axis=0).astype(bf16)


def call(kernel, name, out_shape, in_specs, scratch, flops, moved):
    return pl.pallas_call(
        kernel,
        name=name,
        out_shape=out_shape,
        in_specs=in_specs,
        out_specs=jax.tree.map(lambda _: VMEM, out_shape),
        scratch_shapes=scratch,
        compiler_params=pltpu.CompilerParams(vmem_limit_bytes=40 * 2**20),
        cost_estimate=pl.CostEstimate(flops=flops, bytes_accessed=moved, transcendentals=0),
    )


def to_rows(array):
    slots, width = array.shape
    return array.reshape(slots, width // LANE, LANE).transpose(1, 0, 2).reshape(-1, LANE)


def from_rows(rows, slots):
    return rows.reshape(-1, slots, LANE).transpose(1, 0, 2).reshape(slots, -1)


def body(
    grad_query,
    grad_key,
    weight_query,
    weight_key,
    moment_query,
    moment_key,
    logit_peak,
    owner_table,
    head_order,
):
    owners = lax.axis_size("dp")
    ranks = lax.axis_size("mp")
    devices = owners * ranks
    layers, heads, piece_q = grad_query.shape
    piece_k = grad_key.shape[2]
    slots = moment_query.shape[0]
    per_rank = heads // ranks
    tiles = (piece_q + piece_k) // LANE
    kw = dict(ranks=ranks, owners=owners, slots=slots)
    shape = jax.ShapeDtypeStruct
    owner_2d = owner_table[:, :, 0]
    owner_1d = owner_2d.reshape(-1)
    head_row = head_order.reshape(1, heads)

    packed = call(
        functools.partial(pack_grads_kernel, **kw),
        "pack_grads",
        shape((devices * tiles * slots, LANE), bf16),
        [VMEM] * 4,
        [pltpu.VMEM((devices * tiles * slots, LANE), f32)],
        2 * 256 * 128 * 2816,
        3 * 2**20,
    )(
        owner_2d,
        head_row,
        grad_query.reshape(layers * heads, piece_q),
        grad_key.reshape(layers * heads, piece_k),
    )
    packed = packed.reshape(devices, tiles, slots, LANE).transpose(0, 2, 1, 3).reshape(devices, slots, -1)
    owned = lax.all_to_all(packed, ("dp", "mp"), split_axis=0, concat_axis=0, tiled=True)
    owned = owned.reshape(devices, slots, tiles, LANE).transpose(0, 2, 1, 3).reshape(-1, LANE)

    wrows = layers * tiles * per_rank
    packed_w = call(
        functools.partial(pack_weights_kernel, ranks=ranks),
        "pack_weights",
        shape((ranks * wrows, LANE), bf16),
        [VMEM] * 3,
        [pltpu.VMEM((ranks * wrows, LANE), f32)],
        2 * 128 * 64 * 2816,
        3 * 2**20,
    )(head_row, weight_query, weight_key)
    weights = lax.all_to_all(
        packed_w.reshape(ranks, wrows, LANE), "mp", split_axis=0, concat_axis=0, tiled=True
    )

    fq = DQ * RQ // LANE
    fk = DN * RK // LANE
    send_rows = slots * (fq + fk) // owners + 16
    polar, next_q, next_k = call(
        functools.partial(polar_kernel, **kw),
        "polar",
        (
            shape((owners, send_rows, LANE), bf16),
            shape((fq * slots, LANE), f32),
            shape((fk * slots, LANE), f32),
        ),
        [SMEM, VMEM, VMEM, VMEM, VMEM],
        [pltpu.VMEM((fq, LANE), f32), pltpu.VMEM((fk, LANE), f32)],
        4 * 10**9,
        8 * 2**20,
    )(owner_1d, owned, to_rows(moment_query), to_rows(moment_key), logit_peak[0])
    back = lax.all_to_all(polar, "dp", split_axis=0, concat_axis=0, tiled=True)

    oq = layers * per_rank * fq // owners
    ok = layers * per_rank * fk // owners
    new_q, new_k = call(
        functools.partial(finish_kernel, **kw),
        "finish",
        (shape((oq, LANE), bf16), shape((ok, LANE), bf16)),
        [SMEM, SMEM, VMEM, VMEM],
        [pltpu.VMEM((oq, LANE), f32), pltpu.VMEM((ok, LANE), f32)],
        10**7,
        4 * 2**20,
    )(owner_1d, head_order, back, weights)

    def rollout(rows):
        rows = rows.reshape(layers, -1, per_rank, LANE).transpose(0, 2, 1, 3)
        return rows.reshape(layers, per_rank, -1)

    return rollout(new_q), rollout(new_k), from_rows(next_q, slots), from_rows(next_k, slots)


def solution(mesh):
    placed = (
        P(None, None, ("dp", "mp")),
        P(None, None, ("dp", "mp")),
        P(None, None, ("dp", "mp")),
        P(None, None, ("dp", "mp")),
        P(("dp", "mp"), None),
        P(("dp", "mp"), None),
        P("dp", None, None),
        P(),
        P(),
    )
    return jax.shard_map(
        body,
        mesh=mesh,
        in_specs=placed,
        out_specs=(
            P(None, "mp", "dp"),
            P(None, "mp", "dp"),
            P(("dp", "mp"), None),
            P(("dp", "mp"), None),
        ),
        check_vma=False,
    )
```

```python
import functools
import math

import jax
import jax.numpy as jnp
from jax import lax
from jax.experimental import pallas as pl
from jax.experimental.pallas import tpu as pltpu
from jax.sharding import PartitionSpec as P

DN = 128
RQ = 1536
RK = 512
ITERS = 5
DQ = 192
LANE = 128

quintic_one = 3.4445
quintic_two = -4.775
quintic_three = 2.0315
momentum_decay = 0.95
step_size = 0.5
logit_cap = 100.0

f32 = jnp.float32
bf16 = jnp.bfloat16
VMEM = pl.BlockSpec(memory_space=pltpu.VMEM)
SMEM = pl.BlockSpec(memory_space=pltpu.SMEM)
HBM = pl.BlockSpec(memory_space=pltpu.HBM)
SIDE = 4


def iota(shape, dim):
    return lax.broadcasted_iota(jnp.int32, shape, dim)


def dot(a, b, dims=((1,), (0,))):
    return lax.dot_general(a, b, (dims, ((), ())), preferred_element_type=f32)


def head_matrix(head_ref, heads):
    return (iota((heads, heads), 0) == head_ref[...]).astype(bf16)


def pack_grads_kernel(
    owner_ref, head_ref, gq_far, gk_far, out_far, gq_ref, gk_ref, stage, out_ref, sems, *, ranks, owners, slots
):
    copies = [
        pltpu.make_async_copy(gq_far, gq_ref, sems.at[0]),
        pltpu.make_async_copy(gk_far, gk_ref, sems.at[1]),
    ]
    for copy in copies:
        copy.start()
    layers, heads = owner_ref.shape
    devices = ranks * owners
    per_rank = heads // ranks
    tq = gq_ref.shape[1] // LANE
    tk = gk_ref.shape[1] // LANE
    rows = (tq + tk) * slots
    by_lane = owner_ref[...].astype(f32)
    eye = (iota((heads, heads), 0) == iota((heads, heads), 1)).astype(f32)
    by_row = dot(eye, by_lane, ((1,), (1,)))
    other, mine = iota((heads, heads), 0), iota((heads, heads), 1)
    same_rank = (other // per_rank) == (mine // per_rank)
    heads_of = head_matrix(head_ref, heads)
    lane_rank = iota((1, heads), 1) // per_rank
    picks = [[None] * layers for _ in range(slots)]
    for layer in range(layers):
        owner = by_lane[layer : layer + 1, :]
        earlier = jnp.zeros((1, heads), f32)
        for before in range(layers):
            ahead = (other <= mine) if before < layer else (other < mine)
            hit = same_rank & ahead & (by_row[:, before : before + 1] == owner)
            earlier += jnp.sum(hit.astype(f32), axis=0, keepdims=True)
        target = (owner.astype(jnp.int32) * ranks + lane_rank) * slots + earlier.astype(jnp.int32)
        for slot in range(slots):
            chosen = (iota((devices, heads), 0) * slots + slot == target).astype(bf16)
            picks[slot][layer] = dot(chosen, heads_of, ((1,), (1,))).astype(bf16)
    for copy in copies:
        copy.wait()
    for slot in range(slots):
        pick = jnp.concatenate(picks[slot], axis=1)
        for ref, tiles, base in ((gq_ref, tq, 0), (gk_ref, tk, tq)):
            value = dot(pick, ref[...])
            for tile in range(tiles):
                stage[pl.ds((base + tile) * slots + slot, devices, stride=rows), :] = value[
                    :, tile * LANE : (tile + 1) * LANE
                ]
    sends = []
    count = out_ref.shape[0] // owners
    for owner in range(owners):
        at = pl.ds(owner * count, count)
        out_ref[at, :] = stage[at, :].astype(bf16)
        sends.append(pltpu.make_async_copy(out_ref.at[at, :], out_far.at[at, :], sems.at[2 + owner]))
        sends[-1].start()
    for copy in sends:
        copy.wait()


def pack_weights_kernel(head_ref, wq_ref, wk_ref, *rest, ranks):
    outs, stage = rest[:-1], rest[-1]
    here_rank = lax.axis_index("mp")
    here_x, here_y = here_rank // SIDE, here_rank % SIDE
    layers, heads, _ = wq_ref.shape
    per_rank = heads // ranks
    tq = wq_ref.shape[2] // LANE
    tk = wk_ref.shape[2] // LANE
    rows = layers * (tq + tk) * per_rank
    heads_of = head_matrix(head_ref, heads)
    place, position = iota((heads, heads), 0), iota((heads, heads), 1)
    to_x = (here_x + place % SIDE) % SIDE
    to_y = (here_y + place % ranks // SIDE) % SIDE
    order = (position == (to_x * SIDE + to_y) * per_rank + place // ranks).astype(bf16)
    pick = dot(order, heads_of, ((1,), (1,))).astype(bf16)
    for layer in range(layers):
        for ref, tiles, base in ((wq_ref, tq, 0), (wk_ref, tk, tq)):
            value = dot(pick, ref[layer])
            for tile in range(tiles):
                first = (layer * (tq + tk) + base + tile) * per_rank
                for place_in in range(per_rank):
                    stage[pl.ds(first + place_in, ranks, stride=rows), :] = value[
                        place_in * ranks : (place_in + 1) * ranks, tile * LANE : (tile + 1) * LANE
                    ]
    for shift, out in enumerate(outs):
        out[...] = stage[shift * SIDE * rows : (shift + 1) * SIDE * rows, :].astype(bf16).reshape(SIDE, rows, LANE)


def polar_kernel(
    owner_ref,
    recv_ref,
    mq_far,
    mk_far,
    out_far,
    mq_next,
    mk_next,
    mq_ref,
    mk_ref,
    out_ref,
    sems_in,
    sems_out,
    sems_send,
    *,
    ranks,
    owners,
    slots,
):
    devices = ranks * owners
    parts = sems_in.shape[0] // 2

    def piece(ref, part):
        count = ref.shape[0] // parts
        return ref.at[pl.ds(part * count, count), :]

    def moves(sems, pairs):
        return [
            [
                pltpu.make_async_copy(piece(src, part), piece(dst, part), sems.at[2 * part + j])
                for j, (src, dst) in enumerate(pairs)
            ]
            for part in range(parts)
        ]

    loads = moves(sems_in, ((mq_far, mq_ref), (mk_far, mk_ref)))
    stores = moves(sems_out, ((mq_ref, mq_next), (mk_ref, mk_next)))
    for pair in loads:
        for copy in pair:
            copy.start()
    here_owner = lax.axis_index("dp")
    here_rank = lax.axis_index("mp")
    layers, heads = owner_ref.shape
    per_rank = heads // ranks
    named = (owner_ref[...] == here_owner) & (iota((layers, heads), 1) // per_rank == here_rank)
    held = jnp.sum(jnp.sum(named.astype(f32), axis=1, keepdims=True), axis=0, keepdims=True)
    held = jnp.broadcast_to(held.astype(jnp.int32), (8, LANE))
    sub = iota((8, LANE), 0)
    decay = jnp.where((sub % slots) < held, momentum_decay, 1.0)
    low = sub < 4
    tq = DQ * RQ // LANE // devices * slots
    tk = DN * RK // LANE // devices * slots
    rows = tq + tk

    def tile_of(value, index):
        return value[index * 8 : (index + 1) * 8, :]

    def step(quad, totals):
        totals = list(totals)
        block = recv_ref[pl.ds(pl.multiple_of(quad * 4 * rows, 16), 4 * rows), :].astype(f32)
        for pair in range(2):
            g = [tile_of(block, pair * 11 + j) for j in range(11)]
            query = g[0:4] + [jnp.where(low, g[4], g[5])] + g[6:10]
            key = [pltpu.roll(jnp.where(low, g[5], g[4]), 4, 0), g[10]]
            for which, (grads, ref, count) in enumerate(((query, mq_ref, 9), (key, mk_ref, 2))):
                base = pl.multiple_of((quad * 2 + pair) * count * 8, 8)
                for j in range(count):
                    at = pl.ds(pl.multiple_of(base + j * 8, 8), 8)
                    new = ref[at, :] * decay + grads[j]
                    ref[at, :] = new
                    totals[which] += new * new
        return tuple(totals)

    totals = (jnp.zeros((8, LANE), f32), jnp.zeros((8, LANE), f32))
    turns = devices // 4 // parts
    for part in range(parts):
        for copy in loads[part]:
            copy.wait()
        totals = lax.fori_loop(part * turns, (part + 1) * turns, step, totals)
        for copy in stores[part]:
            copy.start()

    chains = []
    for slot in range(slots):
        for ref, total, height, width in ((mq_ref, totals[0], DQ, RQ), (mk_ref, totals[1], DN, RK)):
            tiles = width // LANE
            norm = jnp.sqrt(jnp.sum(jnp.where(sub % slots == slot, total, 0.0), keepdims=True))
            scale = 1.0 / (norm + 1e-07)
            chains.append(
                jnp.concatenate(
                    [
                        (ref[pl.ds(tile * slots + slot, height, stride=tiles * slots), :] * scale).astype(bf16)
                        for tile in range(tiles)
                    ],
                    axis=1,
                )
            )
    for turn in range(ITERS):
        grams = [dot(x, x, ((1,), (1,))).astype(bf16) for x in chains]
        squares = [dot(a, a) for a in grams]
        mixings = [
            (quintic_two * a.astype(f32) + quintic_three * s).astype(bf16) for a, s in zip(grams, squares)
        ]
        products = [dot(b, x) for b, x in zip(mixings, chains)]
        chains = [quintic_one * x.astype(f32) + y for x, y in zip(chains, products)]
        if turn < ITERS - 1:
            chains = [x.astype(bf16) for x in chains]
    fq = DQ * RQ // LANE // owners
    fk = DN * RK // LANE // owners
    sends = []
    for owner in range(owners):
        for slot in range(slots):
            for x, height, width, at in (
                (chains[2 * slot], DQ, RQ, slot * (fq + fk)),
                (chains[2 * slot + 1], DN, RK, slot * (fq + fk) + fq),
            ):
                span = height // owners
                mine = x[owner * span : (owner + 1) * span]
                for tile in range(0, width // LANE, 2):
                    both = [mine[:, (tile + j) * LANE : (tile + j + 1) * LANE] for j in range(2)]
                    out_ref[owner, at + tile * span : at + (tile + 2) * span, :] = jnp.concatenate(
                        both, axis=0
                    ).astype(bf16)
        sends.append(pltpu.make_async_copy(out_ref.at[owner], out_far.at[owner], sems_send.at[owner]))
        sends[-1].start()
    for copy in sends:
        copy.wait()
    for pair in stores:
        for copy in pair:
            copy.wait()


def finish_kernel(owner_ref, head_ref, peak_ref, polar_ref, *rest, ranks, owners, slots):
    weight_refs, (q_out, k_out, spread_q, spread_k) = rest[:SIDE], rest[SIDE:]
    here_owner = lax.axis_index("dp")
    here_rank = lax.axis_index("mp")
    heads = head_ref.shape[0]
    layers = owner_ref.shape[0]
    per_rank = heads // ranks
    fq = DQ * RQ // LANE // owners
    fk = DN * RK // LANE // owners
    peaks = jnp.concatenate([peak_ref[...].astype(f32), jnp.zeros((layers, LANE - heads), f32)], axis=1)
    names = [
        owner_ref[layer, here_rank * per_rank + place] for place in range(per_rank) for layer in range(layers)
    ]
    sub, lane = iota((8, LANE), 0), iota((8, LANE), 1)
    head_of = jnp.zeros((8, LANE), jnp.int32)
    for place in range(per_rank):
        head_of = jnp.where(sub % per_rank == place, head_ref[here_rank * per_rank + place], head_of)
    sq = fq // ranks * per_rank
    sk = fk // ranks * per_rank
    span = sq + sk
    cq = step_size * 0.2 * math.sqrt(max(DQ, RQ))
    ck = step_size * 0.2 * math.sqrt(max(DN, RK))
    for layer in range(layers):
        for place in range(per_rank):
            unit = place * layers + layer
            earlier = jnp.int32(0)
            for before in range(unit):
                earlier += (names[before] == names[unit]).astype(jnp.int32)
            start = pl.multiple_of(earlier * (fq + fk), 16)
            block = polar_ref[names[unit], pl.ds(start, fq + fk), :].astype(f32)
            for spread, height, width, base in ((spread_q, DQ, RQ, 0), (spread_k, DN, RK, fq)):
                deep = height // owners
                tiles = width // LANE
                first = layer * deep * tiles * per_rank + place
                for tile in range(tiles):
                    spread[pl.ds(first + tile * per_rank, deep, stride=tiles * per_rank), :] = block[
                        base + tile * deep : base + (tile + 1) * deep
                    ]
    for t in range(SIDE):
        for s in range(SIDE):
            source = (here_rank // SIDE + SIDE - t) % SIDE * SIDE + (here_rank % SIDE + SIDE - s) % SIDE
            held = weight_refs[t][s].astype(f32)
            for layer in range(layers):
                at = pl.ds(pl.multiple_of(layer * fq * per_rank + source * sq, 8), sq)
                spread_q[at, :] = held[layer * span : layer * span + sq] - cq * spread_q[at, :]
                at = pl.ds(pl.multiple_of(layer * fk * per_rank + source * sk, 8), sk)
                spread_k[at, :] = held[layer * span + sq : (layer + 1) * span] - ck * spread_k[at, :]
    for layer in range(layers):
        peak = jnp.sum(
            jnp.where(head_of == lane, jnp.broadcast_to(peaks[layer : layer + 1, :], (8, LANE)), 0.0),
            axis=1,
            keepdims=True,
        )
        factor = jnp.broadcast_to(jnp.minimum(1.0, logit_cap / peak), (8, LANE))
        root = jnp.sqrt(factor)
        height = RQ // LANE * per_rank
        for row in range(DQ // owners):
            at = layer * fq * per_rank + row * height
            scale = jnp.where(here_owner * (DQ // owners) + row < DN, root, factor)
            value = spread_q[at : at + height, :] * jnp.concatenate([scale] * (height // 8), axis=0)
            q_out[at : at + height, :] = value.astype(bf16)
        at = layer * fk * per_rank
        height = fk * per_rank
        value = spread_k[at : at + height, :] * jnp.concatenate([root] * (height // 8), axis=0)
        k_out[at : at + height, :] = value.astype(bf16)


def call(kernel, name, out_shape, in_specs, scratch, flops, moved, out_specs=None, limit=8):
    return pl.pallas_call(
        kernel,
        name=name,
        out_shape=out_shape,
        in_specs=in_specs,
        out_specs=out_specs or jax.tree.map(lambda _: VMEM, out_shape),
        scratch_shapes=scratch,
        compiler_params=pltpu.CompilerParams(vmem_limit_bytes=limit * 2**20),
        cost_estimate=pl.CostEstimate(flops=flops, bytes_accessed=moved, transcendentals=0),
    )


def to_rows(array):
    slots, width = array.shape
    return array.reshape(slots, width // LANE, LANE).transpose(1, 0, 2).reshape(-1, LANE)


def from_rows(rows, slots):
    return rows.reshape(-1, slots, LANE).transpose(1, 0, 2).reshape(slots, -1)


def body(
    grad_query,
    grad_key,
    weight_query,
    weight_key,
    moment_query,
    moment_key,
    logit_peak,
    owner_table,
    head_order,
):
    owners = lax.axis_size("dp")
    ranks = lax.axis_size("mp")
    devices = owners * ranks
    layers, heads, piece_q = grad_query.shape
    piece_k = grad_key.shape[2]
    slots = moment_query.shape[0]
    per_rank = heads // ranks
    tiles = (piece_q + piece_k) // LANE
    kw = dict(ranks=ranks, owners=owners, slots=slots)
    shape = jax.ShapeDtypeStruct
    owner_2d = owner_table[:, :, 0].T
    head_row = head_order.reshape(1, heads)

    packed = call(
        functools.partial(pack_grads_kernel, **kw),
        "pack_grads",
        shape((devices * tiles * slots, LANE), bf16),
        [VMEM, VMEM, HBM, HBM],
        [
            pltpu.VMEM((layers * heads, piece_q), bf16),
            pltpu.VMEM((layers * heads, piece_k), bf16),
            pltpu.VMEM((devices * tiles * slots, LANE), f32),
            pltpu.VMEM((devices * tiles * slots, LANE), bf16),
            pltpu.SemaphoreType.DMA((2 + owners,)),
        ],
        2 * 256 * 128 * 2816,
        3 * 2**20,
        out_specs=HBM,
        limit=58,
    )(
        owner_2d,
        head_row,
        grad_query.reshape(layers * heads, piece_q),
        grad_key.reshape(layers * heads, piece_k),
    )
    packed = packed.reshape(devices, tiles, slots, LANE).transpose(0, 2, 1, 3).reshape(devices, slots, -1)
    owned = lax.all_to_all(packed, ("dp", "mp"), split_axis=0, concat_axis=0, tiled=True)
    owned = owned.reshape(devices, slots, tiles, LANE).transpose(0, 2, 1, 3).reshape(-1, LANE)

    wrows = layers * tiles * per_rank
    by_y = call(
        functools.partial(pack_weights_kernel, ranks=ranks),
        "pack_weights",
        [shape((SIDE, wrows, LANE), bf16)] * SIDE,
        [VMEM] * 3,
        [pltpu.VMEM((ranks * wrows, LANE), f32)],
        2 * 128 * 64 * 2816,
        3 * 2**20,
    )(head_row, weight_query, weight_key)
    along_y = [
        [(i, i // SIDE * SIDE + (i + s) % SIDE) for i in range(ranks)] for s in range(SIDE)
    ]
    along_x = [[(i, (i + t * SIDE) % ranks) for i in range(ranks)] for t in range(SIDE)]
    peaks = logit_peak[0]
    reach = 1
    while reach < owners:
        peaks = jnp.maximum(peaks, lax.ppermute(peaks, "dp", [(i, i ^ reach) for i in range(owners)]))
        reach *= 2
    owned, by_y, peaks = lax.optimization_barrier((owned, by_y, peaks))
    by_y = [by_y[0]] + [lax.ppermute(by_y[s], "mp", along_y[s]) for s in range(1, SIDE)]
    fq = DQ * RQ // LANE
    fk = DN * RK // LANE
    parts = 4
    polar, next_q, next_k = call(
        functools.partial(polar_kernel, **kw),
        "polar",
        (
            shape((owners, slots * (fq + fk) // owners, LANE), bf16),
            shape((fq * slots, LANE), f32),
            shape((fk * slots, LANE), f32),
        ),
        [VMEM, VMEM, HBM, HBM],
        [
            pltpu.VMEM((fq * slots, LANE), f32),
            pltpu.VMEM((fk * slots, LANE), f32),
            pltpu.VMEM((owners, slots * (fq + fk) // owners, LANE), bf16),
            pltpu.SemaphoreType.DMA((2 * parts,)),
            pltpu.SemaphoreType.DMA((2 * parts,)),
            pltpu.SemaphoreType.DMA((owners,)),
        ],
        4 * 10**9,
        8 * 2**20,
        (HBM, HBM, HBM),
        50,
    )(owner_2d, owned, to_rows(moment_query), to_rows(moment_key))
    polar, by_y = lax.optimization_barrier((polar, by_y))
    by_x = [jnp.stack([block[t] for block in by_y], axis=0) for t in range(SIDE)]
    weights = [by_x[0]] + [lax.ppermute(by_x[t], "mp", along_x[t]) for t in range(1, SIDE)]
    back = lax.all_to_all(polar, "dp", split_axis=0, concat_axis=0, tiled=True)

    oq = layers * per_rank * fq // owners
    ok = layers * per_rank * fk // owners
    new_q, new_k = call(
        functools.partial(finish_kernel, **kw),
        "finish",
        (shape((oq, LANE), bf16), shape((ok, LANE), bf16)),
        [SMEM, SMEM, VMEM, VMEM] + [VMEM] * SIDE,
        [
            pltpu.VMEM((oq, LANE), f32),
            pltpu.VMEM((ok, LANE), f32),
        ],
        10**7,
        4 * 2**20,
    )(owner_2d, head_order, peaks, back, *weights)

    def rollout(rows):
        rows = rows.reshape(layers, -1, per_rank, LANE).transpose(0, 2, 1, 3)
        return rows.reshape(layers, per_rank, -1)

    return rollout(new_q), rollout(new_k), from_rows(next_q, slots), from_rows(next_k, slots)


def solution(mesh):
    placed = (
        P(None, None, ("dp", "mp")),
        P(None, None, ("dp", "mp")),
        P(None, None, ("dp", "mp")),
        P(None, None, ("dp", "mp")),
        P(("dp", "mp"), None),
        P(("dp", "mp"), None),
        P("dp", None, None),
        P(),
        P(),
    )
    return jax.shard_map(
        body,
        mesh=mesh,
        in_specs=placed,
        out_specs=(
            P(None, "mp", "dp"),
            P(None, "mp", "dp"),
            P(("dp", "mp"), None),
            P(("dp", "mp"), None),
        ),
        check_vma=False,
    )
```

```python
import functools
import math

import jax
import jax.numpy as jnp
from jax import lax
from jax.experimental import pallas as pl
from jax.experimental.pallas import tpu as pltpu
from jax.sharding import PartitionSpec as P

DN = 128
RQ = 1536
RK = 512
ITERS = 5
DQ = 192
LANE = 128

quintic_one = 3.4445
quintic_two = -4.775
quintic_three = 2.0315
momentum_decay = 0.95
step_size = 0.5
logit_cap = 100.0

f32 = jnp.float32
bf16 = jnp.bfloat16
VMEM = pl.BlockSpec(memory_space=pltpu.VMEM)
SMEM = pl.BlockSpec(memory_space=pltpu.SMEM)
HBM = pl.BlockSpec(memory_space=pltpu.HBM)
SIDE = 4


def iota(shape, dim):
    return lax.broadcasted_iota(jnp.int32, shape, dim)


def dot(a, b, dims=((1,), (0,))):
    return lax.dot_general(a, b, (dims, ((), ())), preferred_element_type=f32)


def head_matrix(head_ref, heads):
    return (iota((heads, heads), 0) == head_ref[...]).astype(bf16)


def pack_grads_kernel(
    owner_ref, head_ref, gq_far, gk_far, out_far, gq_ref, gk_ref, stage, out_ref, sems, *, ranks, owners, slots
):
    copies = [
        pltpu.make_async_copy(gq_far, gq_ref, sems.at[0]),
        pltpu.make_async_copy(gk_far, gk_ref, sems.at[1]),
    ]
    for copy in copies:
        copy.start()
    layers, heads = owner_ref.shape
    devices = ranks * owners
    per_rank = heads // ranks
    tq = gq_ref.shape[1] // LANE
    tk = gk_ref.shape[1] // LANE
    rows = (tq + tk) * slots
    by_lane = owner_ref[...].astype(f32)
    eye = (iota((heads, heads), 0) == iota((heads, heads), 1)).astype(f32)
    by_row = dot(eye, by_lane, ((1,), (1,)))
    other, mine = iota((heads, heads), 0), iota((heads, heads), 1)
    same_rank = (other // per_rank) == (mine // per_rank)
    heads_of = head_matrix(head_ref, heads)
    lane_rank = iota((1, heads), 1) // per_rank
    picks = [[None] * layers for _ in range(slots)]
    for layer in range(layers):
        owner = by_lane[layer : layer + 1, :]
        earlier = jnp.zeros((1, heads), f32)
        for before in range(layers):
            ahead = (other <= mine) if before < layer else (other < mine)
            hit = same_rank & ahead & (by_row[:, before : before + 1] == owner)
            earlier += jnp.sum(hit.astype(f32), axis=0, keepdims=True)
        target = (owner.astype(jnp.int32) * ranks + lane_rank) * slots + earlier.astype(jnp.int32)
        for slot in range(slots):
            chosen = (iota((devices, heads), 0) * slots + slot == target).astype(bf16)
            picks[slot][layer] = dot(chosen, heads_of, ((1,), (1,))).astype(bf16)
    for copy in copies:
        copy.wait()
    for slot in range(slots):
        pick = jnp.concatenate(picks[slot], axis=1)
        for ref, tiles, base in ((gq_ref, tq, 0), (gk_ref, tk, tq)):
            value = dot(pick, ref[...])
            for tile in range(tiles):
                stage[pl.ds((base + tile) * slots + slot, devices, stride=rows), :] = value[
                    :, tile * LANE : (tile + 1) * LANE
                ]
    sends = []
    count = out_ref.shape[0] // owners
    for owner in range(owners):
        at = pl.ds(owner * count, count)
        out_ref[at, :] = stage[at, :].astype(bf16)
        sends.append(pltpu.make_async_copy(out_ref.at[at, :], out_far.at[at, :], sems.at[2 + owner]))
        sends[-1].start()
    for copy in sends:
        copy.wait()


def pack_weights_kernel(head_ref, wq_ref, wk_ref, *rest, ranks):
    outs, stage = rest[:-1], rest[-1]
    here_rank = lax.axis_index("mp")
    here_x, here_y = here_rank // SIDE, here_rank % SIDE
    layers, heads, _ = wq_ref.shape
    per_rank = heads // ranks
    tq = wq_ref.shape[2] // LANE
    tk = wk_ref.shape[2] // LANE
    rows = layers * (tq + tk) * per_rank
    heads_of = head_matrix(head_ref, heads)
    place, position = iota((heads, heads), 0), iota((heads, heads), 1)
    to_x = (here_x + place % SIDE) % SIDE
    to_y = (here_y + place % ranks // SIDE) % SIDE
    order = (position == (to_x * SIDE + to_y) * per_rank + place // ranks).astype(bf16)
    pick = dot(order, heads_of, ((1,), (1,))).astype(bf16)
    for layer in range(layers):
        for ref, tiles, base in ((wq_ref, tq, 0), (wk_ref, tk, tq)):
            value = dot(pick, ref[layer])
            for tile in range(tiles):
                first = (layer * (tq + tk) + base + tile) * per_rank
                for place_in in range(per_rank):
                    stage[pl.ds(first + place_in, ranks, stride=rows), :] = value[
                        place_in * ranks : (place_in + 1) * ranks, tile * LANE : (tile + 1) * LANE
                    ]
    for shift, out in enumerate(outs):
        out[...] = stage[shift * SIDE * rows : (shift + 1) * SIDE * rows, :].astype(bf16).reshape(SIDE, rows, LANE)


def polar_kernel(
    owner_ref,
    recv_ref,
    mq_far,
    mk_far,
    out_far,
    mq_next,
    mk_next,
    mq_ref,
    mk_ref,
    out_ref,
    sems_in,
    sems_out,
    sems_send,
    *,
    ranks,
    owners,
    slots,
):
    devices = ranks * owners
    parts = sems_in.shape[0] // 2

    def piece(ref, part):
        count = ref.shape[0] // parts
        return ref.at[pl.ds(part * count, count), :]

    def moves(sems, pairs):
        return [
            [
                pltpu.make_async_copy(piece(src, part), piece(dst, part), sems.at[2 * part + j])
                for j, (src, dst) in enumerate(pairs)
            ]
            for part in range(parts)
        ]

    loads = moves(sems_in, ((mq_far, mq_ref), (mk_far, mk_ref)))
    stores = moves(sems_out, ((mq_ref, mq_next), (mk_ref, mk_next)))
    for pair in loads:
        for copy in pair:
            copy.start()
    here_owner = lax.axis_index("dp")
    here_rank = lax.axis_index("mp")
    layers, heads = owner_ref.shape
    per_rank = heads // ranks
    named = (owner_ref[...] == here_owner) & (iota((layers, heads), 1) // per_rank == here_rank)
    held = jnp.sum(jnp.sum(named.astype(f32), axis=1, keepdims=True), axis=0, keepdims=True)
    held = jnp.broadcast_to(held.astype(jnp.int32), (8, LANE))
    sub = iota((8, LANE), 0)
    decay = jnp.where((sub % slots) < held, momentum_decay, 1.0)
    low = sub < 4
    tq = DQ * RQ // LANE // devices * slots
    tk = DN * RK // LANE // devices * slots
    rows = tq + tk

    def tile_of(value, index):
        return value[index * 8 : (index + 1) * 8, :]

    def step(quad, totals):
        totals = list(totals)
        block = recv_ref[pl.ds(pl.multiple_of(quad * 4 * rows, 16), 4 * rows), :].astype(f32)
        for pair in range(2):
            g = [tile_of(block, pair * 11 + j) for j in range(11)]
            query = g[0:4] + [jnp.where(low, g[4], g[5])] + g[6:10]
            key = [pltpu.roll(jnp.where(low, g[5], g[4]), 4, 0), g[10]]
            for which, (grads, ref, count) in enumerate(((query, mq_ref, 9), (key, mk_ref, 2))):
                base = pl.multiple_of((quad * 2 + pair) * count * 8, 8)
                for j in range(count):
                    at = pl.ds(pl.multiple_of(base + j * 8, 8), 8)
                    new = ref[at, :] * decay + grads[j]
                    ref[at, :] = new
                    totals[which] += new * new
        return tuple(totals)

    totals = (jnp.zeros((8, LANE), f32), jnp.zeros((8, LANE), f32))
    turns = devices // 4 // parts
    for part in range(parts):
        for copy in loads[part]:
            copy.wait()
        totals = lax.fori_loop(part * turns, (part + 1) * turns, step, totals)
        for copy in stores[part]:
            copy.start()

    chains = []
    for slot in range(slots):
        for ref, total, height, width in ((mq_ref, totals[0], DQ, RQ), (mk_ref, totals[1], DN, RK)):
            tiles = width // LANE
            norm = jnp.sqrt(jnp.sum(jnp.where(sub % slots == slot, total, 0.0), keepdims=True))
            scale = 1.0 / (norm + 1e-07)
            chains.append(
                jnp.concatenate(
                    [
                        (ref[pl.ds(tile * slots + slot, height, stride=tiles * slots), :] * scale).astype(bf16)
                        for tile in range(tiles)
                    ],
                    axis=1,
                )
            )
    for turn in range(ITERS):
        grams = [dot(x, x, ((1,), (1,))).astype(bf16) for x in chains]
        squares = [dot(a, a) for a in grams]
        mixings = [
            (quintic_two * a.astype(f32) + quintic_three * s).astype(bf16) for a, s in zip(grams, squares)
        ]
        products = [dot(b, x) for b, x in zip(mixings, chains)]
        chains = [quintic_one * x.astype(f32) + y for x, y in zip(chains, products)]
        if turn < ITERS - 1:
            chains = [x.astype(bf16) for x in chains]
    fq = DQ * RQ // LANE // owners
    fk = DN * RK // LANE // owners
    sends = []
    for owner in range(owners):
        for slot in range(slots):
            for x, height, width, at in (
                (chains[2 * slot], DQ, RQ, slot * (fq + fk)),
                (chains[2 * slot + 1], DN, RK, slot * (fq + fk) + fq),
            ):
                span = height // owners
                mine = x[owner * span : (owner + 1) * span]
                for tile in range(0, width // LANE, 2):
                    both = [mine[:, (tile + j) * LANE : (tile + j + 1) * LANE] for j in range(2)]
                    out_ref[owner, at + tile * span : at + (tile + 2) * span, :] = jnp.concatenate(
                        both, axis=0
                    ).astype(bf16)
        sends.append(pltpu.make_async_copy(out_ref.at[owner], out_far.at[owner], sems_send.at[owner]))
        sends[-1].start()
    for copy in sends:
        copy.wait()
    for pair in stores:
        for copy in pair:
            copy.wait()


def finish_kernel(owner_ref, head_ref, peak_ref, polar_ref, *rest, ranks, owners, slots):
    weight_refs, (q_out, k_out, spread_q, spread_k) = rest[:SIDE], rest[SIDE:]
    here_owner = lax.axis_index("dp")
    here_rank = lax.axis_index("mp")
    heads = head_ref.shape[0]
    layers = owner_ref.shape[0]
    per_rank = heads // ranks
    fq = DQ * RQ // LANE // owners
    fk = DN * RK // LANE // owners
    peaks = jnp.concatenate([peak_ref[...].astype(f32), jnp.zeros((layers, LANE - heads), f32)], axis=1)
    names = [
        owner_ref[layer, here_rank * per_rank + place] for place in range(per_rank) for layer in range(layers)
    ]
    sub, lane = iota((8, LANE), 0), iota((8, LANE), 1)
    head_of = jnp.zeros((8, LANE), jnp.int32)
    for place in range(per_rank):
        head_of = jnp.where(sub % per_rank == place, head_ref[here_rank * per_rank + place], head_of)
    sq = fq // ranks * per_rank
    sk = fk // ranks * per_rank
    span = sq + sk
    cq = step_size * 0.2 * math.sqrt(max(DQ, RQ))
    ck = step_size * 0.2 * math.sqrt(max(DN, RK))
    for layer in range(layers):
        for place in range(per_rank):
            unit = place * layers + layer
            earlier = jnp.int32(0)
            for before in range(unit):
                earlier += (names[before] == names[unit]).astype(jnp.int32)
            start = pl.multiple_of(earlier * (fq + fk), 16)
            block = polar_ref[names[unit], pl.ds(start, fq + fk), :].astype(f32)
            for spread, height, width, base in ((spread_q, DQ, RQ, 0), (spread_k, DN, RK, fq)):
                deep = height // owners
                tiles = width // LANE
                first = layer * deep * tiles * per_rank + place
                for tile in range(tiles):
                    spread[pl.ds(first + tile * per_rank, deep, stride=tiles * per_rank), :] = block[
                        base + tile * deep : base + (tile + 1) * deep
                    ]
    for t in range(SIDE):
        for s in range(SIDE):
            source = (here_rank // SIDE + SIDE - t) % SIDE * SIDE + (here_rank % SIDE + SIDE - s) % SIDE
            held = weight_refs[t][s].astype(f32)
            for layer in range(layers):
                at = pl.ds(pl.multiple_of(layer * fq * per_rank + source * sq, 8), sq)
                spread_q[at, :] = held[layer * span : layer * span + sq] - cq * spread_q[at, :]
                at = pl.ds(pl.multiple_of(layer * fk * per_rank + source * sk, 8), sk)
                spread_k[at, :] = held[layer * span + sq : (layer + 1) * span] - ck * spread_k[at, :]
    for layer in range(layers):
        peak = jnp.sum(
            jnp.where(head_of == lane, jnp.broadcast_to(peaks[layer : layer + 1, :], (8, LANE)), 0.0),
            axis=1,
            keepdims=True,
        )
        factor = jnp.broadcast_to(jnp.minimum(1.0, logit_cap / peak), (8, LANE))
        root = jnp.sqrt(factor)
        height = RQ // LANE * per_rank
        for row in range(DQ // owners):
            at = layer * fq * per_rank + row * height
            scale = jnp.where(here_owner * (DQ // owners) + row < DN, root, factor)
            value = spread_q[at : at + height, :] * jnp.concatenate([scale] * (height // 8), axis=0)
            q_out[at : at + height, :] = value.astype(bf16)
        at = layer * fk * per_rank
        height = fk * per_rank
        value = spread_k[at : at + height, :] * jnp.concatenate([root] * (height // 8), axis=0)
        k_out[at : at + height, :] = value.astype(bf16)


def call(kernel, name, out_shape, in_specs, scratch, flops, moved, out_specs=None, limit=8):
    return pl.pallas_call(
        kernel,
        name=name,
        out_shape=out_shape,
        in_specs=in_specs,
        out_specs=out_specs or jax.tree.map(lambda _: VMEM, out_shape),
        scratch_shapes=scratch,
        compiler_params=pltpu.CompilerParams(vmem_limit_bytes=limit * 2**20),
        cost_estimate=pl.CostEstimate(flops=flops, bytes_accessed=moved, transcendentals=0),
    )


def to_rows(array):
    slots, width = array.shape
    return array.reshape(slots, width // LANE, LANE).transpose(1, 0, 2).reshape(-1, LANE)


def from_rows(rows, slots):
    return rows.reshape(-1, slots, LANE).transpose(1, 0, 2).reshape(slots, -1)


def body(
    grad_query,
    grad_key,
    weight_query,
    weight_key,
    moment_query,
    moment_key,
    logit_peak,
    owner_table,
    head_order,
):
    owners = lax.axis_size("dp")
    ranks = lax.axis_size("mp")
    devices = owners * ranks
    layers, heads, piece_q = grad_query.shape
    piece_k = grad_key.shape[2]
    slots = moment_query.shape[0]
    per_rank = heads // ranks
    tiles = (piece_q + piece_k) // LANE
    kw = dict(ranks=ranks, owners=owners, slots=slots)
    shape = jax.ShapeDtypeStruct
    owner_2d = owner_table[:, :, 0].T
    head_row = head_order.reshape(1, heads)

    packed = call(
        functools.partial(pack_grads_kernel, **kw),
        "pack_grads",
        shape((devices * tiles * slots, LANE), bf16),
        [VMEM, VMEM, HBM, HBM],
        [
            pltpu.VMEM((layers * heads, piece_q), bf16),
            pltpu.VMEM((layers * heads, piece_k), bf16),
            pltpu.VMEM((devices * tiles * slots, LANE), f32),
            pltpu.VMEM((devices * tiles * slots, LANE), bf16),
            pltpu.SemaphoreType.DMA((2 + owners,)),
        ],
        2 * 256 * 128 * 2816,
        3 * 2**20,
        out_specs=HBM,
        limit=58,
    )(
        owner_2d,
        head_row,
        grad_query.reshape(layers * heads, piece_q),
        grad_key.reshape(layers * heads, piece_k),
    )
    packed = packed.reshape(devices, tiles, slots, LANE).transpose(0, 2, 1, 3).reshape(devices, slots, -1)
    owned = lax.all_to_all(packed, ("dp", "mp"), split_axis=0, concat_axis=0, tiled=True)
    owned = owned.reshape(devices, slots, tiles, LANE).transpose(0, 2, 1, 3).reshape(-1, LANE)

    wrows = layers * tiles * per_rank
    by_y = call(
        functools.partial(pack_weights_kernel, ranks=ranks),
        "pack_weights",
        [shape((SIDE, wrows, LANE), bf16)] * SIDE,
        [VMEM] * 3,
        [pltpu.VMEM((ranks * wrows, LANE), f32)],
        2 * 128 * 64 * 2816,
        3 * 2**20,
    )(head_row, weight_query, weight_key)
    along_y = [
        [(i, i // SIDE * SIDE + (i + s) % SIDE) for i in range(ranks)] for s in range(SIDE)
    ]
    along_x = [[(i, (i + t * SIDE) % ranks) for i in range(ranks)] for t in range(SIDE)]
    peaks = logit_peak[0]
    reach = 1
    while reach < owners:
        peaks = jnp.maximum(peaks, lax.ppermute(peaks, "dp", [(i, i ^ reach) for i in range(owners)]))
        if reach == 2:
            peaks, by_y = lax.optimization_barrier((peaks, by_y))
        reach *= 2
    by_y = [by_y[0]] + [lax.ppermute(by_y[s], "mp", along_y[s]) for s in range(1, SIDE)]
    fq = DQ * RQ // LANE
    fk = DN * RK // LANE
    parts = 4
    polar, next_q, next_k = call(
        functools.partial(polar_kernel, **kw),
        "polar",
        (
            shape((owners, slots * (fq + fk) // owners, LANE), bf16),
            shape((fq * slots, LANE), f32),
            shape((fk * slots, LANE), f32),
        ),
        [VMEM, VMEM, HBM, HBM],
        [
            pltpu.VMEM((fq * slots, LANE), f32),
            pltpu.VMEM((fk * slots, LANE), f32),
            pltpu.VMEM((owners, slots * (fq + fk) // owners, LANE), bf16),
            pltpu.SemaphoreType.DMA((2 * parts,)),
            pltpu.SemaphoreType.DMA((2 * parts,)),
            pltpu.SemaphoreType.DMA((owners,)),
        ],
        4 * 10**9,
        8 * 2**20,
        (HBM, HBM, HBM),
        50,
    )(owner_2d, owned, to_rows(moment_query), to_rows(moment_key))
    polar, by_y = lax.optimization_barrier((polar, by_y))
    by_x = [jnp.stack([block[t] for block in by_y], axis=0) for t in range(SIDE)]
    weights = [by_x[0]] + [lax.ppermute(by_x[t], "mp", along_x[t]) for t in range(1, SIDE)]
    back = lax.all_to_all(polar, "dp", split_axis=0, concat_axis=0, tiled=True)

    oq = layers * per_rank * fq // owners
    ok = layers * per_rank * fk // owners
    new_q, new_k = call(
        functools.partial(finish_kernel, **kw),
        "finish",
        (shape((oq, LANE), bf16), shape((ok, LANE), bf16)),
        [SMEM, SMEM, VMEM, VMEM] + [VMEM] * SIDE,
        [
            pltpu.VMEM((oq, LANE), f32),
            pltpu.VMEM((ok, LANE), f32),
        ],
        10**7,
        4 * 2**20,
    )(owner_2d, head_order, peaks, back, *weights)

    def rollout(rows):
        rows = rows.reshape(layers, -1, per_rank, LANE).transpose(0, 2, 1, 3)
        return rows.reshape(layers, per_rank, -1)

    return rollout(new_q), rollout(new_k), from_rows(next_q, slots), from_rows(next_k, slots)


def solution(mesh):
    placed = (
        P(None, None, ("dp", "mp")),
        P(None, None, ("dp", "mp")),
        P(None, None, ("dp", "mp")),
        P(None, None, ("dp", "mp")),
        P(("dp", "mp"), None),
        P(("dp", "mp"), None),
        P("dp", None, None),
        P(),
        P(),
    )
    return jax.shard_map(
        body,
        mesh=mesh,
        in_specs=placed,
        out_specs=(
            P(None, "mp", "dp"),
            P(None, "mp", "dp"),
            P(("dp", "mp"), None),
            P(("dp", "mp"), None),
        ),
        check_vma=False,
    )
```

```python
import functools
import math

import jax
import jax.numpy as jnp
from jax import lax
from jax.experimental import pallas as pl
from jax.experimental.pallas import tpu as pltpu
from jax.sharding import PartitionSpec as P

DN = 128
RQ = 1536
RK = 512
ITERS = 5
DQ = 192
LANE = 128

quintic_one = 3.4445
quintic_two = -4.775
quintic_three = 2.0315
momentum_decay = 0.95
step_size = 0.5
logit_cap = 100.0

f32 = jnp.float32
bf16 = jnp.bfloat16
VMEM = pl.BlockSpec(memory_space=pltpu.VMEM)
SMEM = pl.BlockSpec(memory_space=pltpu.SMEM)
HBM = pl.BlockSpec(memory_space=pltpu.HBM)
SIDE = 4


def iota(shape, dim):
    return lax.broadcasted_iota(jnp.int32, shape, dim)


def dot(a, b, dims=((1,), (0,))):
    return lax.dot_general(a, b, (dims, ((), ())), preferred_element_type=f32)


def head_matrix(head_ref, heads):
    return (iota((heads, heads), 0) == head_ref[...]).astype(bf16)


def pack_grads_kernel(
    owner_far,
    head_far,
    gq_far,
    gk_far,
    out_far,
    owner_ref,
    head_ref,
    gq_ref,
    gk_ref,
    stage,
    out_ref,
    sems,
    sems_send,
    *,
    ranks,
    owners,
    slots,
):
    copies = [
        pltpu.make_async_copy(src, dst, sems.at[j])
        for j, (src, dst) in enumerate(
            ((owner_far, owner_ref), (head_far, head_ref), (gq_far, gq_ref), (gk_far, gk_ref))
        )
    ]
    for copy in copies:
        copy.start()
    for copy in copies[:2]:
        copy.wait()
    layers, heads = owner_ref.shape
    devices = ranks * owners
    per_rank = heads // ranks
    tq = gq_ref.shape[1] // LANE
    tk = gk_ref.shape[1] // LANE
    rows = (tq + tk) * slots
    by_lane = owner_ref[...].astype(f32)
    eye = (iota((heads, heads), 0) == iota((heads, heads), 1)).astype(f32)
    by_row = dot(eye, by_lane, ((1,), (1,)))
    other, mine = iota((heads, heads), 0), iota((heads, heads), 1)
    same_rank = (other // per_rank) == (mine // per_rank)
    heads_of = head_matrix(head_ref, heads)
    lane_rank = iota((1, heads), 1) // per_rank
    picks = [[None] * layers for _ in range(slots)]
    for layer in range(layers):
        owner = by_lane[layer : layer + 1, :]
        earlier = jnp.zeros((1, heads), f32)
        for before in range(layers):
            ahead = (other <= mine) if before < layer else (other < mine)
            hit = same_rank & ahead & (by_row[:, before : before + 1] == owner)
            earlier += jnp.sum(hit.astype(f32), axis=0, keepdims=True)
        target = (owner.astype(jnp.int32) * ranks + lane_rank) * slots + earlier.astype(jnp.int32)
        for slot in range(slots):
            chosen = (iota((devices, heads), 0) * slots + slot == target).astype(bf16)
            picks[slot][layer] = dot(chosen, heads_of, ((1,), (1,))).astype(bf16)
    for copy in copies[2:]:
        copy.wait()
    for slot in range(slots):
        pick = jnp.concatenate(picks[slot], axis=1)
        for ref, tiles, base in ((gq_ref, tq, 0), (gk_ref, tk, tq)):
            value = dot(pick, ref[...])
            for tile in range(tiles):
                stage[pl.ds((base + tile) * slots + slot, devices, stride=rows), :] = value[
                    :, tile * LANE : (tile + 1) * LANE
                ]
    sends = []
    parts = sems_send.shape[0]
    count = out_ref.shape[0] // parts
    for part in range(parts):
        at = pl.ds(part * count, count)
        out_ref[at, :] = stage[at, :].astype(bf16)
        sends.append(pltpu.make_async_copy(out_ref.at[at, :], out_far.at[at, :], sems_send.at[part]))
        sends[-1].start()
    for copy in sends:
        copy.wait()


def pack_weights_kernel(head_ref, wq_ref, wk_ref, *rest, ranks):
    outs, stage = rest[:-1], rest[-1]
    here_rank = lax.axis_index("mp")
    here_x, here_y = here_rank // SIDE, here_rank % SIDE
    layers, heads, _ = wq_ref.shape
    per_rank = heads // ranks
    tq = wq_ref.shape[2] // LANE
    tk = wk_ref.shape[2] // LANE
    rows = layers * (tq + tk) * per_rank
    heads_of = head_matrix(head_ref, heads)
    place, position = iota((heads, heads), 0), iota((heads, heads), 1)
    to_x = (here_x + place % SIDE) % SIDE
    to_y = (here_y + place % ranks // SIDE) % SIDE
    order = (position == (to_x * SIDE + to_y) * per_rank + place // ranks).astype(bf16)
    pick = dot(order, heads_of, ((1,), (1,))).astype(bf16)
    for layer in range(layers):
        for ref, tiles, base in ((wq_ref, tq, 0), (wk_ref, tk, tq)):
            value = dot(pick, ref[layer])
            for tile in range(tiles):
                first = (layer * (tq + tk) + base + tile) * per_rank
                for place_in in range(per_rank):
                    stage[pl.ds(first + place_in, ranks, stride=rows), :] = value[
                        place_in * ranks : (place_in + 1) * ranks, tile * LANE : (tile + 1) * LANE
                    ]
    for shift, out in enumerate(outs):
        out[...] = stage[shift * SIDE * rows : (shift + 1) * SIDE * rows, :].astype(bf16).reshape(SIDE, rows, LANE)


def polar_kernel(
    owner_ref,
    recv_ref,
    mq_far,
    mk_far,
    out_far,
    mq_next,
    mk_next,
    mq_ref,
    mk_ref,
    out_ref,
    sems_in,
    sems_out,
    sems_send,
    *,
    ranks,
    owners,
    slots,
):
    devices = ranks * owners
    parts = sems_in.shape[0] // 2

    def piece(ref, part):
        count = ref.shape[0] // parts
        return ref.at[pl.ds(part * count, count), :]

    def moves(sems, pairs):
        return [
            [
                pltpu.make_async_copy(piece(src, part), piece(dst, part), sems.at[2 * part + j])
                for j, (src, dst) in enumerate(pairs)
            ]
            for part in range(parts)
        ]

    loads = moves(sems_in, ((mq_far, mq_ref), (mk_far, mk_ref)))
    stores = moves(sems_out, ((mq_ref, mq_next), (mk_ref, mk_next)))
    for pair in loads:
        for copy in pair:
            copy.start()
    here_owner = lax.axis_index("dp")
    here_rank = lax.axis_index("mp")
    layers, heads = owner_ref.shape
    per_rank = heads // ranks
    named = (owner_ref[...] == here_owner) & (iota((layers, heads), 1) // per_rank == here_rank)
    held = jnp.sum(jnp.sum(named.astype(f32), axis=1, keepdims=True), axis=0, keepdims=True)
    held = jnp.broadcast_to(held.astype(jnp.int32), (8, LANE))
    sub = iota((8, LANE), 0)
    decay = jnp.where((sub % slots) < held, momentum_decay, 1.0)
    low = sub < 4
    tq = DQ * RQ // LANE // devices * slots
    tk = DN * RK // LANE // devices * slots
    rows = tq + tk

    def tile_of(value, index):
        return value[index * 8 : (index + 1) * 8, :]

    def step(quad, totals):
        totals = list(totals)
        block = recv_ref[pl.ds(pl.multiple_of(quad * 4 * rows, 16), 4 * rows), :].astype(f32)
        for pair in range(2):
            g = [tile_of(block, pair * 11 + j) for j in range(11)]
            query = g[0:4] + [jnp.where(low, g[4], g[5])] + g[6:10]
            key = [pltpu.roll(jnp.where(low, g[5], g[4]), 4, 0), g[10]]
            for which, (grads, ref, count) in enumerate(((query, mq_ref, 9), (key, mk_ref, 2))):
                base = pl.multiple_of((quad * 2 + pair) * count * 8, 8)
                for j in range(count):
                    at = pl.ds(pl.multiple_of(base + j * 8, 8), 8)
                    new = ref[at, :] * decay + grads[j]
                    ref[at, :] = new
                    totals[which] += new * new
        return tuple(totals)

    totals = (jnp.zeros((8, LANE), f32), jnp.zeros((8, LANE), f32))
    turns = devices // 4 // parts
    for part in range(parts):
        for copy in loads[part]:
            copy.wait()
        totals = lax.fori_loop(part * turns, (part + 1) * turns, step, totals)
        for copy in stores[part]:
            copy.start()

    chains = []
    for slot in range(slots):
        for ref, total, height, width in ((mq_ref, totals[0], DQ, RQ), (mk_ref, totals[1], DN, RK)):
            tiles = width // LANE
            norm = jnp.sqrt(jnp.sum(jnp.where(sub % slots == slot, total, 0.0), keepdims=True))
            scale = 1.0 / (norm + 1e-07)
            chains.append(
                jnp.concatenate(
                    [
                        (ref[pl.ds(tile * slots + slot, height, stride=tiles * slots), :] * scale).astype(bf16)
                        for tile in range(tiles)
                    ],
                    axis=1,
                )
            )
    for turn in range(ITERS):
        grams = [dot(x, x, ((1,), (1,))).astype(bf16) for x in chains]
        squares = [dot(a, a) for a in grams]
        mixings = [
            (quintic_two * a.astype(f32) + quintic_three * s).astype(bf16) for a, s in zip(grams, squares)
        ]
        products = [dot(b, x) for b, x in zip(mixings, chains)]
        chains = [quintic_one * x.astype(f32) + y for x, y in zip(chains, products)]
        if turn < ITERS - 1:
            chains = [x.astype(bf16) for x in chains]
    fq = DQ * RQ // LANE // owners
    fk = DN * RK // LANE // owners
    sends = []
    for owner in range(owners):
        for slot in range(slots):
            for x, height, width, at in (
                (chains[2 * slot], DQ, RQ, slot * (fq + fk)),
                (chains[2 * slot + 1], DN, RK, slot * (fq + fk) + fq),
            ):
                span = height // owners
                mine = x[owner * span : (owner + 1) * span]
                for tile in range(0, width // LANE, 2):
                    both = [mine[:, (tile + j) * LANE : (tile + j + 1) * LANE] for j in range(2)]
                    out_ref[owner, at + tile * span : at + (tile + 2) * span, :] = jnp.concatenate(
                        both, axis=0
                    ).astype(bf16)
        sends.append(pltpu.make_async_copy(out_ref.at[owner], out_far.at[owner], sems_send.at[owner]))
        sends[-1].start()
    for copy in sends:
        copy.wait()
    for pair in stores:
        for copy in pair:
            copy.wait()


def finish_kernel(owner_ref, head_ref, peak_ref, polar_ref, *rest, ranks, owners, slots):
    weight_refs, (q_out, k_out, spread_q, spread_k) = rest[:SIDE], rest[SIDE:]
    here_owner = lax.axis_index("dp")
    here_rank = lax.axis_index("mp")
    heads = head_ref.shape[0]
    layers = owner_ref.shape[0]
    per_rank = heads // ranks
    fq = DQ * RQ // LANE // owners
    fk = DN * RK // LANE // owners
    peaks = jnp.concatenate([peak_ref[...].astype(f32), jnp.zeros((layers, LANE - heads), f32)], axis=1)
    names = [
        owner_ref[layer, here_rank * per_rank + place] for place in range(per_rank) for layer in range(layers)
    ]
    sub, lane = iota((8, LANE), 0), iota((8, LANE), 1)
    head_of = jnp.zeros((8, LANE), jnp.int32)
    for place in range(per_rank):
        head_of = jnp.where(sub % per_rank == place, head_ref[here_rank * per_rank + place], head_of)
    sq = fq // ranks * per_rank
    sk = fk // ranks * per_rank
    span = sq + sk
    cq = step_size * 0.2 * math.sqrt(max(DQ, RQ))
    ck = step_size * 0.2 * math.sqrt(max(DN, RK))
    for layer in range(layers):
        for place in range(per_rank):
            unit = place * layers + layer
            earlier = jnp.int32(0)
            for before in range(unit):
                earlier += (names[before] == names[unit]).astype(jnp.int32)
            start = pl.multiple_of(earlier * (fq + fk), 16)
            block = polar_ref[names[unit], pl.ds(start, fq + fk), :].astype(f32)
            for spread, height, width, base in ((spread_q, DQ, RQ, 0), (spread_k, DN, RK, fq)):
                deep = height // owners
                tiles = width // LANE
                first = layer * deep * tiles * per_rank + place
                for tile in range(tiles):
                    spread[pl.ds(first + tile * per_rank, deep, stride=tiles * per_rank), :] = block[
                        base + tile * deep : base + (tile + 1) * deep
                    ]
    for t in range(SIDE):
        for s in range(SIDE):
            source = (here_rank // SIDE + SIDE - t) % SIDE * SIDE + (here_rank % SIDE + SIDE - s) % SIDE
            held = weight_refs[t][s].astype(f32)
            for layer in range(layers):
                at = pl.ds(pl.multiple_of(layer * fq * per_rank + source * sq, 8), sq)
                spread_q[at, :] = held[layer * span : layer * span + sq] - cq * spread_q[at, :]
                at = pl.ds(pl.multiple_of(layer * fk * per_rank + source * sk, 8), sk)
                spread_k[at, :] = held[layer * span + sq : (layer + 1) * span] - ck * spread_k[at, :]
    for layer in range(layers):
        peak = jnp.sum(
            jnp.where(head_of == lane, jnp.broadcast_to(peaks[layer : layer + 1, :], (8, LANE)), 0.0),
            axis=1,
            keepdims=True,
        )
        factor = jnp.broadcast_to(jnp.minimum(1.0, logit_cap / peak), (8, LANE))
        root = jnp.sqrt(factor)
        height = RQ // LANE * per_rank
        for row in range(DQ // owners):
            at = layer * fq * per_rank + row * height
            scale = jnp.where(here_owner * (DQ // owners) + row < DN, root, factor)
            value = spread_q[at : at + height, :] * jnp.concatenate([scale] * (height // 8), axis=0)
            q_out[at : at + height, :] = value.astype(bf16)
        at = layer * fk * per_rank
        height = fk * per_rank
        value = spread_k[at : at + height, :] * jnp.concatenate([root] * (height // 8), axis=0)
        k_out[at : at + height, :] = value.astype(bf16)


def call(kernel, name, out_shape, in_specs, scratch, flops, moved, out_specs=None, limit=8):
    return pl.pallas_call(
        kernel,
        name=name,
        out_shape=out_shape,
        in_specs=in_specs,
        out_specs=out_specs or jax.tree.map(lambda _: VMEM, out_shape),
        scratch_shapes=scratch,
        compiler_params=pltpu.CompilerParams(vmem_limit_bytes=limit * 2**20),
        cost_estimate=pl.CostEstimate(flops=flops, bytes_accessed=moved, transcendentals=0),
    )


def to_rows(array):
    slots, width = array.shape
    return array.reshape(slots, width // LANE, LANE).transpose(1, 0, 2).reshape(-1, LANE)


def from_rows(rows, slots):
    return rows.reshape(-1, slots, LANE).transpose(1, 0, 2).reshape(slots, -1)


def body(
    grad_query,
    grad_key,
    weight_query,
    weight_key,
    moment_query,
    moment_key,
    logit_peak,
    owner_table,
    head_order,
):
    owners = lax.axis_size("dp")
    ranks = lax.axis_size("mp")
    devices = owners * ranks
    layers, heads, piece_q = grad_query.shape
    piece_k = grad_key.shape[2]
    slots = moment_query.shape[0]
    per_rank = heads // ranks
    tiles = (piece_q + piece_k) // LANE
    kw = dict(ranks=ranks, owners=owners, slots=slots)
    shape = jax.ShapeDtypeStruct
    owner_2d = owner_table[:, :, 0].T
    head_row = head_order.reshape(1, heads)

    packed = call(
        functools.partial(pack_grads_kernel, **kw),
        "pack_grads",
        shape((devices * tiles * slots, LANE), bf16),
        [HBM] * 4,
        [
            pltpu.VMEM(owner_2d.shape, jnp.int32),
            pltpu.VMEM(head_row.shape, jnp.int32),
            pltpu.VMEM((layers * heads, piece_q), bf16),
            pltpu.VMEM((layers * heads, piece_k), bf16),
            pltpu.VMEM((devices * tiles * slots, LANE), f32),
            pltpu.VMEM((devices * tiles * slots, LANE), bf16),
            pltpu.SemaphoreType.DMA((4,)),
            pltpu.SemaphoreType.DMA((4,)),
        ],
        2 * 256 * 128 * 2816,
        3 * 2**20,
        out_specs=HBM,
        limit=58,
    )(
        owner_2d,
        head_row,
        grad_query.reshape(layers * heads, piece_q),
        grad_key.reshape(layers * heads, piece_k),
    )
    packed = packed.reshape(devices, tiles, slots, LANE).transpose(0, 2, 1, 3).reshape(devices, slots, -1)
    owned = lax.all_to_all(packed, ("dp", "mp"), split_axis=0, concat_axis=0, tiled=True)
    owned = owned.reshape(devices, slots, tiles, LANE).transpose(0, 2, 1, 3).reshape(-1, LANE)

    wrows = layers * tiles * per_rank
    by_y = call(
        functools.partial(pack_weights_kernel, ranks=ranks),
        "pack_weights",
        [shape((SIDE, wrows, LANE), bf16)] * SIDE,
        [VMEM] * 3,
        [pltpu.VMEM((ranks * wrows, LANE), f32)],
        2 * 128 * 64 * 2816,
        3 * 2**20,
    )(head_row, weight_query, weight_key)
    along_y = [
        [(i, i // SIDE * SIDE + (i + s) % SIDE) for i in range(ranks)] for s in range(SIDE)
    ]
    along_x = [[(i, (i + t * SIDE) % ranks) for i in range(ranks)] for t in range(SIDE)]
    peaks = logit_peak[0]
    for reach in (1, 4, 2):
        peaks = jnp.maximum(peaks, lax.ppermute(peaks, "dp", [(i, i ^ reach) for i in range(owners)]))
        if reach == 4:
            peaks, by_y = lax.optimization_barrier((peaks, by_y))
    by_y = [by_y[0]] + [lax.ppermute(by_y[s], "mp", along_y[s]) for s in range(1, SIDE)]
    fq = DQ * RQ // LANE
    fk = DN * RK // LANE
    parts = 2
    polar, next_q, next_k = call(
        functools.partial(polar_kernel, **kw),
        "polar",
        (
            shape((owners, slots * (fq + fk) // owners, LANE), bf16),
            shape((fq * slots, LANE), f32),
            shape((fk * slots, LANE), f32),
        ),
        [VMEM, VMEM, HBM, HBM],
        [
            pltpu.VMEM((fq * slots, LANE), f32),
            pltpu.VMEM((fk * slots, LANE), f32),
            pltpu.VMEM((owners, slots * (fq + fk) // owners, LANE), bf16),
            pltpu.SemaphoreType.DMA((2 * parts,)),
            pltpu.SemaphoreType.DMA((2 * parts,)),
            pltpu.SemaphoreType.DMA((owners,)),
        ],
        4 * 10**9,
        8 * 2**20,
        (HBM, HBM, HBM),
        50,
    )(owner_2d, owned, to_rows(moment_query), to_rows(moment_key))
    polar, by_y = lax.optimization_barrier((polar, by_y))
    by_x = [jnp.stack([block[t] for block in by_y], axis=0) for t in range(SIDE)]
    weights = [by_x[0]] + [lax.ppermute(by_x[t], "mp", along_x[t]) for t in range(1, SIDE)]
    back = lax.all_to_all(polar, "dp", split_axis=0, concat_axis=0, tiled=True)

    oq = layers * per_rank * fq // owners
    ok = layers * per_rank * fk // owners
    new_q, new_k = call(
        functools.partial(finish_kernel, **kw),
        "finish",
        (shape((oq, LANE), bf16), shape((ok, LANE), bf16)),
        [SMEM, SMEM, VMEM, VMEM] + [VMEM] * SIDE,
        [
            pltpu.VMEM((oq, LANE), f32),
            pltpu.VMEM((ok, LANE), f32),
        ],
        10**7,
        4 * 2**20,
    )(owner_2d, head_order, peaks, back, *weights)

    def rollout(rows):
        rows = rows.reshape(layers, -1, per_rank, LANE).transpose(0, 2, 1, 3)
        return rows.reshape(layers, per_rank, -1)

    return rollout(new_q), rollout(new_k), from_rows(next_q, slots), from_rows(next_k, slots)


def solution(mesh):
    placed = (
        P(None, None, ("dp", "mp")),
        P(None, None, ("dp", "mp")),
        P(None, None, ("dp", "mp")),
        P(None, None, ("dp", "mp")),
        P(("dp", "mp"), None),
        P(("dp", "mp"), None),
        P("dp", None, None),
        P(),
        P(),
    )
    return jax.shard_map(
        body,
        mesh=mesh,
        in_specs=placed,
        out_specs=(
            P(None, "mp", "dp"),
            P(None, "mp", "dp"),
            P(("dp", "mp"), None),
            P(("dp", "mp"), None),
        ),
        check_vma=False,
    )
```

```python
import functools
import math

import jax
import jax.numpy as jnp
from jax import lax
from jax.experimental import pallas as pl
from jax.experimental.pallas import tpu as pltpu
from jax.sharding import PartitionSpec as P

DN = 128
RQ = 1536
RK = 512
ITERS = 5
DQ = 192
LANE = 128

quintic_one = 3.4445
quintic_two = -4.775
quintic_three = 2.0315
momentum_decay = 0.95
step_size = 0.5
logit_cap = 100.0

f32 = jnp.float32
bf16 = jnp.bfloat16
VMEM = pl.BlockSpec(memory_space=pltpu.VMEM)
SMEM = pl.BlockSpec(memory_space=pltpu.SMEM)
HBM = pl.BlockSpec(memory_space=pltpu.HBM)
SIDE = 4


def iota(shape, dim):
    return lax.broadcasted_iota(jnp.int32, shape, dim)


def dot(a, b, dims=((1,), (0,))):
    return lax.dot_general(a, b, (dims, ((), ())), preferred_element_type=f32)


def head_matrix(head_ref, heads):
    return (iota((heads, heads), 0) == head_ref[...]).astype(bf16)


def pack_grads_kernel(
    owner_far,
    head_far,
    gq_far,
    gk_far,
    out_far,
    owner_ref,
    head_ref,
    gq_ref,
    gk_ref,
    stage,
    out_ref,
    sems,
    sems_send,
    *,
    ranks,
    owners,
    slots,
):
    copies = [
        pltpu.make_async_copy(src, dst, sems.at[j])
        for j, (src, dst) in enumerate(
            ((owner_far, owner_ref), (head_far, head_ref), (gq_far, gq_ref), (gk_far, gk_ref))
        )
    ]
    for copy in copies:
        copy.start()
    for copy in copies[:2]:
        copy.wait()
    layers, heads = owner_ref.shape
    devices = ranks * owners
    per_rank = heads // ranks
    tq = gq_ref.shape[1] // LANE
    tk = gk_ref.shape[1] // LANE
    rows = (tq + tk) * slots
    by_lane = owner_ref[...].astype(f32)
    eye = (iota((heads, heads), 0) == iota((heads, heads), 1)).astype(f32)
    by_row = dot(eye, by_lane, ((1,), (1,)))
    other, mine = iota((heads, heads), 0), iota((heads, heads), 1)
    same_rank = (other // per_rank) == (mine // per_rank)
    heads_of = head_matrix(head_ref, heads)
    lane_rank = iota((1, heads), 1) // per_rank
    picks = [[None] * layers for _ in range(slots)]
    for layer in range(layers):
        owner = by_lane[layer : layer + 1, :]
        earlier = jnp.zeros((1, heads), f32)
        for before in range(layers):
            ahead = (other <= mine) if before < layer else (other < mine)
            hit = same_rank & ahead & (by_row[:, before : before + 1] == owner)
            earlier += jnp.sum(hit.astype(f32), axis=0, keepdims=True)
        target = (owner.astype(jnp.int32) * ranks + lane_rank) * slots + earlier.astype(jnp.int32)
        for slot in range(slots):
            chosen = (iota((devices, heads), 0) * slots + slot == target).astype(bf16)
            picks[slot][layer] = dot(chosen, heads_of, ((1,), (1,))).astype(bf16)
    for copy in copies[2:]:
        copy.wait()
    pick = jnp.concatenate([jnp.concatenate(row, axis=1) for row in picks], axis=0)
    for ref, tiles, base in ((gk_ref, tk, tq), (gq_ref, tq, 0)):
        value = dot(pick, ref[...])
        for tile in range(tiles):
            for slot in range(slots):
                stage[pl.ds((base + tile) * slots + slot, devices, stride=rows), :] = value[
                    slot * devices : (slot + 1) * devices, tile * LANE : (tile + 1) * LANE
                ]
    sends = []
    parts = sems_send.shape[0]
    count = out_ref.shape[0] // parts
    for part in range(parts):
        at = pl.ds(part * count, count)
        out_ref[at, :] = stage[at, :].astype(bf16)
        sends.append(pltpu.make_async_copy(out_ref.at[at, :], out_far.at[at, :], sems_send.at[part]))
        sends[-1].start()
    for copy in sends:
        copy.wait()


def pack_weights_kernel(head_ref, wq_ref, wk_ref, *rest, ranks):
    outs, stage = rest[:-1], rest[-1]
    here_rank = lax.axis_index("mp")
    here_x, here_y = here_rank // SIDE, here_rank % SIDE
    layers, heads, _ = wq_ref.shape
    per_rank = heads // ranks
    tq = wq_ref.shape[2] // LANE
    tk = wk_ref.shape[2] // LANE
    rows = layers * (tq + tk) * per_rank
    heads_of = head_matrix(head_ref, heads)
    place, position = iota((heads, heads), 0), iota((heads, heads), 1)
    to_x = (here_x + place % SIDE) % SIDE
    to_y = (here_y + place % ranks // SIDE) % SIDE
    order = (position == (to_x * SIDE + to_y) * per_rank + place // ranks).astype(bf16)
    pick = dot(order, heads_of, ((1,), (1,))).astype(bf16)
    for layer in range(layers):
        for ref, tiles, base in ((wq_ref, tq, 0), (wk_ref, tk, tq)):
            value = dot(pick, ref[layer])
            for tile in range(tiles):
                first = (layer * (tq + tk) + base + tile) * per_rank
                for place_in in range(per_rank):
                    stage[pl.ds(first + place_in, ranks, stride=rows), :] = value[
                        place_in * ranks : (place_in + 1) * ranks, tile * LANE : (tile + 1) * LANE
                    ]
    for shift, out in enumerate(outs):
        out[...] = stage[shift * SIDE * rows : (shift + 1) * SIDE * rows, :].astype(bf16).reshape(SIDE, rows, LANE)


def polar_kernel(
    owner_ref,
    recv_ref,
    mq_far,
    mk_far,
    out_far,
    mq_next,
    mk_next,
    mq_ref,
    mk_ref,
    out_ref,
    sems_in,
    sems_out,
    sem_send,
    *,
    ranks,
    owners,
    slots,
):
    devices = ranks * owners
    parts = sems_in.shape[0] // 2

    def piece(ref, rows, part):
        count = rows // parts
        return ref.at[pl.ds(part * count, count), :]

    def moves(sems, pairs):
        return [
            [
                pltpu.make_async_copy(piece(src, rows, part), piece(dst, rows, part), sems.at[2 * part + j])
                for j, (src, dst, rows) in enumerate(pairs)
            ]
            for part in range(parts)
        ]

    nq, nk = mq_far.shape[0], mk_far.shape[0]
    loads = moves(sems_in, ((mq_far, mq_ref, nq), (mk_far, mk_ref, nk)))
    stores = moves(sems_out, ((mq_ref, mq_next, nq), (mk_ref, mk_next, nk)))
    for pair in loads:
        for copy in pair:
            copy.start()
    here_owner = lax.axis_index("dp")
    here_rank = lax.axis_index("mp")
    layers, heads = owner_ref.shape
    per_rank = heads // ranks
    named = (owner_ref[...] == here_owner) & (iota((layers, heads), 1) // per_rank == here_rank)
    held = jnp.sum(jnp.sum(named.astype(f32), axis=1, keepdims=True), axis=0, keepdims=True)
    held = jnp.broadcast_to(held.astype(jnp.int32), (8, LANE))
    sub = iota((8, LANE), 0)
    decay = jnp.where((sub % slots) < held, momentum_decay, 1.0)
    low = sub < 4
    tq = DQ * RQ // LANE // devices * slots
    tk = DN * RK // LANE // devices * slots
    rows = tq + tk

    def tile_of(value, index):
        return value[index * 8 : (index + 1) * 8, :]

    def step(quad, totals):
        totals = list(totals)
        block = recv_ref[pl.ds(pl.multiple_of(quad * 4 * rows, 16), 4 * rows), :].astype(f32)
        for pair in range(2):
            g = [tile_of(block, pair * 11 + j) for j in range(11)]
            query = g[0:4] + [jnp.where(low, g[4], g[5])] + g[6:10]
            key = [pltpu.roll(jnp.where(low, g[5], g[4]), 4, 0), g[10]]
            for which, (grads, ref, count) in enumerate(((query, mq_ref, 9), (key, mk_ref, 2))):
                base = pl.multiple_of((quad * 2 + pair) * count * 8, 8)
                for j in range(count):
                    at = pl.ds(pl.multiple_of(base + j * 8, 8), 8)
                    new = ref[at, :] * decay + grads[j]
                    ref[at, :] = new
                    totals[which] += new * new
        return tuple(totals)

    totals = (jnp.zeros((8, LANE), f32), jnp.zeros((8, LANE), f32))
    turns = devices // 4 // parts
    for part in range(parts):
        for copy in loads[part]:
            copy.wait()
        totals = lax.fori_loop(part * turns, (part + 1) * turns, step, totals)
        for copy in stores[part]:
            copy.start()

    chains = []
    for slot in range(slots):
        for ref, total, height, width in ((mq_ref, totals[0], DQ, RQ), (mk_ref, totals[1], DN, RK)):
            tiles = width // LANE
            norm = jnp.sqrt(jnp.sum(jnp.where(sub % slots == slot, total, 0.0), keepdims=True))
            scale = 1.0 / (norm + 1e-07)
            chains.append(
                jnp.concatenate(
                    [
                        (ref[pl.ds(tile * slots + slot, height, stride=tiles * slots), :] * scale).astype(bf16)
                        for tile in range(tiles)
                    ],
                    axis=1,
                )
            )
    for turn in range(ITERS):
        grams = [dot(x, x, ((1,), (1,))).astype(bf16) for x in chains]
        squares = [dot(a, a) for a in grams]
        mixings = [
            (quintic_two * a.astype(f32) + quintic_three * s).astype(bf16) for a, s in zip(grams, squares)
        ]
        products = [dot(b, x) for b, x in zip(mixings, chains)]
        chains = [quintic_one * x.astype(f32) + y for x, y in zip(chains, products)]
        if turn < ITERS - 1:
            chains = [x.astype(bf16) for x in chains]
    fq = DQ * RQ // LANE // owners
    fk = DN * RK // LANE // owners
    for owner in range(owners):
        for slot in range(slots):
            for x, height, width, at in (
                (chains[2 * slot], DQ, RQ, slot * (fq + fk)),
                (chains[2 * slot + 1], DN, RK, slot * (fq + fk) + fq),
            ):
                span = height // owners
                mine = x[owner * span : (owner + 1) * span]
                for tile in range(0, width // LANE, 2):
                    both = [mine[:, (tile + j) * LANE : (tile + j + 1) * LANE] for j in range(2)]
                    out_ref[owner, at + tile * span : at + (tile + 2) * span, :] = jnp.concatenate(
                        both, axis=0
                    ).astype(bf16)
    send = pltpu.make_async_copy(out_ref, out_far, sem_send)
    send.start()
    send.wait()
    for pair in stores:
        for copy in pair:
            copy.wait()


def finish_kernel(owner_ref, head_ref, peak_ref, polar_ref, *rest, ranks, owners, slots):
    weight_refs, (q_out, k_out, spread_q, spread_k) = rest[:SIDE], rest[SIDE:]
    here_owner = lax.axis_index("dp")
    here_rank = lax.axis_index("mp")
    heads = head_ref.shape[0]
    layers = owner_ref.shape[0]
    per_rank = heads // ranks
    fq = DQ * RQ // LANE // owners
    fk = DN * RK // LANE // owners
    peaks = jnp.concatenate([peak_ref[...].astype(f32), jnp.zeros((layers, LANE - heads), f32)], axis=1)
    names = [
        owner_ref[layer, here_rank * per_rank + place] for place in range(per_rank) for layer in range(layers)
    ]
    sub, lane = iota((8, LANE), 0), iota((8, LANE), 1)
    head_of = jnp.zeros((8, LANE), jnp.int32)
    for place in range(per_rank):
        head_of = jnp.where(sub % per_rank == place, head_ref[here_rank * per_rank + place], head_of)
    sq = fq // ranks * per_rank
    sk = fk // ranks * per_rank
    span = sq + sk
    cq = step_size * 0.2 * math.sqrt(max(DQ, RQ))
    ck = step_size * 0.2 * math.sqrt(max(DN, RK))
    for layer in range(layers):
        for place in range(per_rank):
            unit = place * layers + layer
            earlier = jnp.int32(0)
            for before in range(unit):
                earlier += (names[before] == names[unit]).astype(jnp.int32)
            start = pl.multiple_of(earlier * (fq + fk), 16)
            block = polar_ref[names[unit], pl.ds(start, fq + fk), :].astype(f32)
            for spread, height, width, base in ((spread_q, DQ, RQ, 0), (spread_k, DN, RK, fq)):
                deep = height // owners
                tiles = width // LANE
                first = layer * deep * tiles * per_rank + place
                for tile in range(tiles):
                    spread[pl.ds(first + tile * per_rank, deep, stride=tiles * per_rank), :] = block[
                        base + tile * deep : base + (tile + 1) * deep
                    ]
    for t in range(SIDE):
        for s in range(SIDE):
            source = (here_rank // SIDE + SIDE - t) % SIDE * SIDE + (here_rank % SIDE + SIDE - s) % SIDE
            held = weight_refs[t][s].astype(f32)
            for layer in range(layers):
                at = pl.ds(pl.multiple_of(layer * fq * per_rank + source * sq, 8), sq)
                spread_q[at, :] = held[layer * span : layer * span + sq] - cq * spread_q[at, :]
                at = pl.ds(pl.multiple_of(layer * fk * per_rank + source * sk, 8), sk)
                spread_k[at, :] = held[layer * span + sq : (layer + 1) * span] - ck * spread_k[at, :]
    for layer in range(layers):
        peak = jnp.sum(
            jnp.where(head_of == lane, jnp.broadcast_to(peaks[layer : layer + 1, :], (8, LANE)), 0.0),
            axis=1,
            keepdims=True,
        )
        factor = jnp.broadcast_to(jnp.minimum(1.0, logit_cap / peak), (8, LANE))
        root = jnp.sqrt(factor)
        height = RQ // LANE * per_rank
        for row in range(DQ // owners):
            at = layer * fq * per_rank + row * height
            scale = jnp.where(here_owner * (DQ // owners) + row < DN, root, factor)
            value = spread_q[at : at + height, :] * jnp.concatenate([scale] * (height // 8), axis=0)
            q_out[at : at + height, :] = value.astype(bf16)
        at = layer * fk * per_rank
        height = fk * per_rank
        value = spread_k[at : at + height, :] * jnp.concatenate([root] * (height // 8), axis=0)
        k_out[at : at + height, :] = value.astype(bf16)


def call(kernel, name, out_shape, in_specs, scratch, flops, moved, out_specs=None, limit=8):
    return pl.pallas_call(
        kernel,
        name=name,
        out_shape=out_shape,
        in_specs=in_specs,
        out_specs=out_specs or jax.tree.map(lambda _: VMEM, out_shape),
        scratch_shapes=scratch,
        compiler_params=pltpu.CompilerParams(vmem_limit_bytes=limit * 2**20),
        cost_estimate=pl.CostEstimate(flops=flops, bytes_accessed=moved, transcendentals=0),
    )


def to_rows(array):
    slots, width = array.shape
    return array.reshape(slots, width // LANE, LANE).transpose(1, 0, 2).reshape(-1, LANE)


def from_rows(rows, slots):
    return rows.reshape(-1, slots, LANE).transpose(1, 0, 2).reshape(slots, -1)


def body(
    grad_query,
    grad_key,
    weight_query,
    weight_key,
    moment_query,
    moment_key,
    logit_peak,
    owner_table,
    head_order,
):
    owners = lax.axis_size("dp")
    ranks = lax.axis_size("mp")
    devices = owners * ranks
    layers, heads, piece_q = grad_query.shape
    piece_k = grad_key.shape[2]
    slots = moment_query.shape[0]
    per_rank = heads // ranks
    tiles = (piece_q + piece_k) // LANE
    kw = dict(ranks=ranks, owners=owners, slots=slots)
    shape = jax.ShapeDtypeStruct
    owner_2d = owner_table[:, :, 0].T
    head_row = head_order.reshape(1, heads)

    packed = call(
        functools.partial(pack_grads_kernel, **kw),
        "pack_grads",
        shape((devices * tiles * slots, LANE), bf16),
        [HBM] * 4,
        [
            pltpu.VMEM(owner_2d.shape, jnp.int32),
            pltpu.VMEM(head_row.shape, jnp.int32),
            pltpu.VMEM((layers * heads, piece_q), bf16),
            pltpu.VMEM((layers * heads, piece_k), bf16),
            pltpu.VMEM(((devices + 1) * tiles * slots, LANE), f32),
            pltpu.VMEM((devices * tiles * slots, LANE), bf16),
            pltpu.SemaphoreType.DMA((4,)),
            pltpu.SemaphoreType.DMA((4,)),
        ],
        2 * 256 * 128 * 2816,
        3 * 2**20,
        out_specs=HBM,
        limit=58,
    )(
        owner_2d,
        head_row,
        grad_query.reshape(layers * heads, piece_q),
        grad_key.reshape(layers * heads, piece_k),
    )
    packed = packed.reshape(devices, tiles, slots, LANE).transpose(0, 2, 1, 3).reshape(devices, slots, -1)
    owned = lax.all_to_all(packed, ("dp", "mp"), split_axis=0, concat_axis=0, tiled=True)
    owned = owned.reshape(devices, slots, tiles, LANE).transpose(0, 2, 1, 3).reshape(-1, LANE)

    wrows = layers * tiles * per_rank
    by_y = call(
        functools.partial(pack_weights_kernel, ranks=ranks),
        "pack_weights",
        [shape((SIDE, wrows, LANE), bf16)] * SIDE,
        [VMEM] * 3,
        [pltpu.VMEM(((ranks + 1) * wrows, LANE), f32)],
        2 * 128 * 64 * 2816,
        3 * 2**20,
    )(head_row, weight_query, weight_key)
    along_y = [
        [(i, i // SIDE * SIDE + (i + s) % SIDE) for i in range(ranks)] for s in range(SIDE)
    ]
    along_x = [[(i, (i + t * SIDE) % ranks) for i in range(ranks)] for t in range(SIDE)]
    peaks = logit_peak[0]
    for reach in (4, 1, 2):
        peaks = jnp.maximum(peaks, lax.ppermute(peaks, "dp", [(i, i ^ reach) for i in range(owners)]))
        if reach == 4:
            peaks, by_y = lax.optimization_barrier((peaks, by_y))
    by_y = [by_y[0]] + [lax.ppermute(by_y[s], "mp", along_y[s]) for s in range(1, SIDE)]
    fq = DQ * RQ // LANE
    fk = DN * RK // LANE
    parts = 2
    polar, next_q, next_k = call(
        functools.partial(polar_kernel, **kw),
        "polar",
        (
            shape((owners, slots * (fq + fk) // owners, LANE), bf16),
            shape((fq * slots, LANE), f32),
            shape((fk * slots, LANE), f32),
        ),
        [VMEM, VMEM, HBM, HBM],
        [
            pltpu.VMEM((fq * slots + RQ // LANE * slots, LANE), f32),
            pltpu.VMEM((fk * slots + RK // LANE * slots, LANE), f32),
            pltpu.VMEM((owners, slots * (fq + fk) // owners, LANE), bf16),
            pltpu.SemaphoreType.DMA((2 * parts,)),
            pltpu.SemaphoreType.DMA((2 * parts,)),
            pltpu.SemaphoreType.DMA,
        ],
        4 * 10**9,
        8 * 2**20,
        (HBM, HBM, HBM),
        50,
    )(owner_2d, owned, to_rows(moment_query), to_rows(moment_key))
    polar, by_y = lax.optimization_barrier((polar, by_y))
    by_x = [jnp.stack([block[t] for block in by_y], axis=0) for t in range(SIDE)]
    weights = [by_x[0]] + [lax.ppermute(by_x[t], "mp", along_x[t]) for t in range(1, SIDE)]
    back = lax.all_to_all(polar, "dp", split_axis=0, concat_axis=0, tiled=True)

    oq = layers * per_rank * fq // owners
    ok = layers * per_rank * fk // owners
    new_q, new_k = call(
        functools.partial(finish_kernel, **kw),
        "finish",
        (shape((oq, LANE), bf16), shape((ok, LANE), bf16)),
        [SMEM, SMEM, VMEM, VMEM] + [VMEM] * SIDE,
        [
            pltpu.VMEM((oq + RQ // LANE * per_rank, LANE), f32),
            pltpu.VMEM((ok + RK // LANE * per_rank, LANE), f32),
        ],
        10**7,
        4 * 2**20,
    )(owner_2d, head_order, peaks, back, *weights)

    def rollout(rows):
        rows = rows.reshape(layers, -1, per_rank, LANE).transpose(0, 2, 1, 3)
        return rows.reshape(layers, per_rank, -1)

    return rollout(new_q), rollout(new_k), from_rows(next_q, slots), from_rows(next_k, slots)


def solution(mesh):
    placed = (
        P(None, None, ("dp", "mp")),
        P(None, None, ("dp", "mp")),
        P(None, None, ("dp", "mp")),
        P(None, None, ("dp", "mp")),
        P(("dp", "mp"), None),
        P(("dp", "mp"), None),
        P("dp", None, None),
        P(),
        P(),
    )
    return jax.shard_map(
        body,
        mesh=mesh,
        in_specs=placed,
        out_specs=(
            P(None, "mp", "dp"),
            P(None, "mp", "dp"),
            P(("dp", "mp"), None),
            P(("dp", "mp"), None),
        ),
        check_vma=False,
    )
```

```python
import functools
import math

import jax
import jax.numpy as jnp
from jax import lax
from jax.experimental import pallas as pl
from jax.experimental.pallas import tpu as pltpu
from jax.sharding import PartitionSpec as P

DN = 128
RQ = 1536
RK = 512
ITERS = 5
DQ = 192
LANE = 128

quintic_one = 3.4445
quintic_two = -4.775
quintic_three = 2.0315
momentum_decay = 0.95
step_size = 0.5
logit_cap = 100.0

f32 = jnp.float32
bf16 = jnp.bfloat16
VMEM = pl.BlockSpec(memory_space=pltpu.VMEM)
SMEM = pl.BlockSpec(memory_space=pltpu.SMEM)
HBM = pl.BlockSpec(memory_space=pltpu.HBM)
SIDE = 4


def iota(shape, dim):
    return lax.broadcasted_iota(jnp.int32, shape, dim)


def dot(a, b, dims=((1,), (0,))):
    return lax.dot_general(a, b, (dims, ((), ())), preferred_element_type=f32)


def head_matrix(head_ref, heads):
    return (iota((heads, heads), 0) == head_ref[...]).astype(bf16)


def pack_grads_kernel(
    owner_far,
    head_far,
    gq_far,
    gk_far,
    out_far,
    owner_ref,
    head_ref,
    gq_ref,
    gk_ref,
    stage,
    out_ref,
    sems,
    sems_send,
    *,
    ranks,
    owners,
    slots,
):
    copies = [
        pltpu.make_async_copy(src, dst, sems.at[j])
        for j, (src, dst) in enumerate(
            ((owner_far, owner_ref), (head_far, head_ref), (gq_far, gq_ref), (gk_far, gk_ref))
        )
    ]
    for copy in copies:
        copy.start()
    for copy in copies[:2]:
        copy.wait()
    layers, heads = owner_ref.shape
    devices = ranks * owners
    per_rank = heads // ranks
    tq = gq_ref.shape[1] // LANE
    tk = gk_ref.shape[1] // LANE
    rows = (tq + tk) * slots
    by_lane = owner_ref[...].astype(f32)
    eye = (iota((heads, heads), 0) == iota((heads, heads), 1)).astype(f32)
    by_row = dot(eye, by_lane, ((1,), (1,)))
    other, mine = iota((heads, heads), 0), iota((heads, heads), 1)
    same_rank = (other // per_rank) == (mine // per_rank)
    heads_of = head_matrix(head_ref, heads)
    lane_rank = iota((1, heads), 1) // per_rank
    picks = [[None] * layers for _ in range(slots)]
    for layer in range(layers):
        owner = by_lane[layer : layer + 1, :]
        earlier = jnp.zeros((1, heads), f32)
        for before in range(layers):
            ahead = (other <= mine) if before < layer else (other < mine)
            hit = same_rank & ahead & (by_row[:, before : before + 1] == owner)
            earlier += jnp.sum(hit.astype(f32), axis=0, keepdims=True)
        target = (owner.astype(jnp.int32) * ranks + lane_rank) * slots + earlier.astype(jnp.int32)
        for slot in range(slots):
            chosen = (iota((devices, heads), 0) * slots + slot == target).astype(bf16)
            picks[slot][layer] = dot(chosen, heads_of, ((1,), (1,))).astype(bf16)
    for copy in copies[2:]:
        copy.wait()
    pick = jnp.concatenate([jnp.concatenate(row, axis=1) for row in picks], axis=0)
    for ref, tiles, base in ((gk_ref, tk, tq), (gq_ref, tq, 0)):
        value = dot(pick, ref[...])
        for tile in range(tiles):
            for slot in range(slots):
                stage[pl.ds((base + tile) * slots + slot, devices, stride=rows), :] = value[
                    slot * devices : (slot + 1) * devices, tile * LANE : (tile + 1) * LANE
                ]
    sends = []
    parts = sems_send.shape[0]
    count = out_ref.shape[0] // parts
    for part in range(parts):
        at = pl.ds(part * count, count)
        out_ref[at, :] = stage[at, :].astype(bf16)
        sends.append(pltpu.make_async_copy(out_ref.at[at, :], out_far.at[at, :], sems_send.at[part]))
        sends[-1].start()
    for copy in sends:
        copy.wait()


def pack_weights_kernel(head_ref, wq_ref, wk_ref, *rest, ranks):
    outs, stage = rest[:-1], rest[-1]
    here_rank = lax.axis_index("mp")
    here_x, here_y = here_rank // SIDE, here_rank % SIDE
    layers, heads, _ = wq_ref.shape
    per_rank = heads // ranks
    tq = wq_ref.shape[2] // LANE
    tk = wk_ref.shape[2] // LANE
    rows = layers * (tq + tk) * per_rank
    heads_of = head_matrix(head_ref, heads)
    place, position = iota((heads, heads), 0), iota((heads, heads), 1)
    to_x = (here_x + place % SIDE) % SIDE
    to_y = (here_y + place % ranks // SIDE) % SIDE
    order = (position == (to_x * SIDE + to_y) * per_rank + place // ranks).astype(bf16)
    pick = dot(order, heads_of, ((1,), (1,))).astype(bf16)
    for layer in range(layers):
        for ref, tiles, base in ((wq_ref, tq, 0), (wk_ref, tk, tq)):
            value = dot(pick, ref[layer])
            for tile in range(tiles):
                first = (layer * (tq + tk) + base + tile) * per_rank
                for place_in in range(per_rank):
                    stage[pl.ds(first + place_in, ranks, stride=rows), :] = value[
                        place_in * ranks : (place_in + 1) * ranks, tile * LANE : (tile + 1) * LANE
                    ]
    for shift, out in enumerate(outs):
        out[...] = stage[shift * SIDE * rows : (shift + 1) * SIDE * rows, :].astype(bf16).reshape(SIDE, rows, LANE)


def polar_kernel(
    owner_ref,
    recv_ref,
    mq_far,
    mk_far,
    out_far,
    mq_next,
    mk_next,
    mq_ref,
    mk_ref,
    gq_ref,
    gk_ref,
    out_ref,
    sems_in,
    sems_out,
    sem_send,
    *,
    ranks,
    owners,
    slots,
):
    devices = ranks * owners
    parts = sems_in.shape[0] // 2

    def piece(ref, rows, part):
        count = rows // parts
        return ref.at[pl.ds(part * count, count), :]

    def moves(sems, pairs):
        return [
            [
                pltpu.make_async_copy(piece(src, rows, part), piece(dst, rows, part), sems.at[2 * part + j])
                for j, (src, dst, rows) in enumerate(pairs)
            ]
            for part in range(parts)
        ]

    nq, nk = mq_far.shape[0], mk_far.shape[0]
    loads = moves(sems_in, ((mq_far, mq_ref, nq), (mk_far, mk_ref, nk)))
    stores = moves(sems_out, ((mq_ref, mq_next, nq), (mk_ref, mk_next, nk)))
    for pair in loads:
        for copy in pair:
            copy.start()
    here_owner = lax.axis_index("dp")
    here_rank = lax.axis_index("mp")
    layers, heads = owner_ref.shape
    per_rank = heads // ranks
    named = (owner_ref[...] == here_owner) & (iota((layers, heads), 1) // per_rank == here_rank)
    held = jnp.sum(jnp.sum(named.astype(f32), axis=1, keepdims=True), axis=0, keepdims=True)
    held = jnp.broadcast_to(held.astype(jnp.int32), (8, LANE))
    sub = iota((8, LANE), 0)
    decay = jnp.where((sub % slots) < held, momentum_decay, 1.0)
    low = sub < 4
    tq = DQ * RQ // LANE // devices * slots
    tk = DN * RK // LANE // devices * slots
    rows = tq + tk

    def tile_of(value, index):
        return value[index * 8 : (index + 1) * 8, :]

    @pl.loop(0, devices // 4)
    def _(quad):
        block = recv_ref[pl.ds(pl.multiple_of(quad * 4 * rows, 16), 4 * rows), :].astype(f32)
        for pair in range(2):
            g = [tile_of(block, pair * 11 + j) for j in range(11)]
            query = g[0:4] + [jnp.where(low, g[4], g[5])] + g[6:10]
            key = [pltpu.roll(jnp.where(low, g[5], g[4]), 4, 0), g[10]]
            for grads, ref in ((query, gq_ref), (key, gk_ref)):
                base = pl.multiple_of((quad * 2 + pair) * len(grads) * 8, 8)
                for j, value in enumerate(grads):
                    ref[pl.ds(pl.multiple_of(base + j * 8, 8), 8), :] = value

    def update(ref, grad_ref, first, count, total):
        span = 128

        def step(index, total):
            at = pl.ds(pl.multiple_of(first + index * span, span), span)
            old, grad = ref[at, :], grad_ref[at, :]
            news = [tile_of(old, j) * decay + tile_of(grad, j) for j in range(span // 8)]
            ref[at, :] = jnp.concatenate(news, axis=0)
            for new in news:
                total = total + new * new
            return total

        return lax.fori_loop(0, count // span, step, total)

    totals = [jnp.zeros((8, LANE), f32)] * 2
    for part in range(parts):
        for copy in loads[part]:
            copy.wait()
        for which, (ref, grad_ref) in enumerate(((mq_ref, gq_ref), (mk_ref, gk_ref))):
            count = grad_ref.shape[0] // parts
            totals[which] = update(ref, grad_ref, part * count, count, totals[which])
        for copy in stores[part]:
            copy.start()

    chains = []
    for slot in range(slots):
        for ref, total, height, width in ((mq_ref, totals[0], DQ, RQ), (mk_ref, totals[1], DN, RK)):
            tiles = width // LANE
            norm = jnp.sqrt(jnp.sum(jnp.where(sub % slots == slot, total, 0.0), keepdims=True))
            scale = 1.0 / (norm + 1e-07)
            chains.append(
                jnp.concatenate(
                    [
                        (ref[pl.ds(tile * slots + slot, height, stride=tiles * slots), :] * scale).astype(bf16)
                        for tile in range(tiles)
                    ],
                    axis=1,
                )
            )
    for turn in range(ITERS):
        grams = [dot(x, x, ((1,), (1,))).astype(bf16) for x in chains]
        squares = [dot(a, a) for a in grams]
        mixings = [
            (quintic_two * a.astype(f32) + quintic_three * s).astype(bf16) for a, s in zip(grams, squares)
        ]
        products = [dot(b, x) for b, x in zip(mixings, chains)]
        chains = [quintic_one * x.astype(f32) + y for x, y in zip(chains, products)]
        if turn < ITERS - 1:
            chains = [x.astype(bf16) for x in chains]
    fq = DQ * RQ // LANE // owners
    fk = DN * RK // LANE // owners
    for owner in range(owners):
        for slot in range(slots):
            for x, height, width, at in (
                (chains[2 * slot], DQ, RQ, slot * (fq + fk)),
                (chains[2 * slot + 1], DN, RK, slot * (fq + fk) + fq),
            ):
                span = height // owners
                mine = x[owner * span : (owner + 1) * span]
                for tile in range(0, width // LANE, 2):
                    both = [mine[:, (tile + j) * LANE : (tile + j + 1) * LANE] for j in range(2)]
                    out_ref[owner, at + tile * span : at + (tile + 2) * span, :] = jnp.concatenate(
                        both, axis=0
                    ).astype(bf16)
    send = pltpu.make_async_copy(out_ref, out_far, sem_send)
    send.start()
    send.wait()
    for pair in stores:
        for copy in pair:
            copy.wait()


def finish_kernel(owner_ref, head_ref, peak_ref, polar_ref, *rest, ranks, owners, slots):
    weight_refs, (q_out, k_out, spread_q, spread_k) = rest[:SIDE], rest[SIDE:]
    here_owner = lax.axis_index("dp")
    here_rank = lax.axis_index("mp")
    heads = head_ref.shape[0]
    layers = owner_ref.shape[0]
    per_rank = heads // ranks
    fq = DQ * RQ // LANE // owners
    fk = DN * RK // LANE // owners
    peaks = jnp.concatenate([peak_ref[...].astype(f32), jnp.zeros((layers, LANE - heads), f32)], axis=1)
    names = [
        owner_ref[layer, here_rank * per_rank + place] for place in range(per_rank) for layer in range(layers)
    ]
    sub, lane = iota((8, LANE), 0), iota((8, LANE), 1)
    head_of = jnp.zeros((8, LANE), jnp.int32)
    for place in range(per_rank):
        head_of = jnp.where(sub % per_rank == place, head_ref[here_rank * per_rank + place], head_of)
    sq = fq // ranks * per_rank
    sk = fk // ranks * per_rank
    span = sq + sk
    cq = step_size * 0.2 * math.sqrt(max(DQ, RQ))
    ck = step_size * 0.2 * math.sqrt(max(DN, RK))
    for layer in range(layers):
        for place in range(per_rank):
            unit = place * layers + layer
            earlier = jnp.int32(0)
            for before in range(unit):
                earlier += (names[before] == names[unit]).astype(jnp.int32)
            start = pl.multiple_of(earlier * (fq + fk), 16)
            block = polar_ref[names[unit], pl.ds(start, fq + fk), :].astype(f32)
            for spread, height, width, base in ((spread_q, DQ, RQ, 0), (spread_k, DN, RK, fq)):
                deep = height // owners
                tiles = width // LANE
                first = layer * deep * tiles * per_rank + place
                for tile in range(tiles):
                    spread[pl.ds(first + tile * per_rank, deep, stride=tiles * per_rank), :] = block[
                        base + tile * deep : base + (tile + 1) * deep
                    ]
    for t in range(SIDE):
        for s in range(SIDE):
            source = (here_rank // SIDE + SIDE - t) % SIDE * SIDE + (here_rank % SIDE + SIDE - s) % SIDE
            held = weight_refs[t][s].astype(f32)
            for layer in range(layers):
                at = pl.ds(pl.multiple_of(layer * fq * per_rank + source * sq, 8), sq)
                spread_q[at, :] = held[layer * span : layer * span + sq] - cq * spread_q[at, :]
                at = pl.ds(pl.multiple_of(layer * fk * per_rank + source * sk, 8), sk)
                spread_k[at, :] = held[layer * span + sq : (layer + 1) * span] - ck * spread_k[at, :]
    for layer in range(layers):
        peak = jnp.sum(
            jnp.where(head_of == lane, jnp.broadcast_to(peaks[layer : layer + 1, :], (8, LANE)), 0.0),
            axis=1,
            keepdims=True,
        )
        factor = jnp.broadcast_to(jnp.minimum(1.0, logit_cap / peak), (8, LANE))
        root = jnp.sqrt(factor)
        height = RQ // LANE * per_rank
        for row in range(DQ // owners):
            at = layer * fq * per_rank + row * height
            scale = jnp.where(here_owner * (DQ // owners) + row < DN, root, factor)
            value = spread_q[at : at + height, :] * jnp.concatenate([scale] * (height // 8), axis=0)
            q_out[at : at + height, :] = value.astype(bf16)
        at = layer * fk * per_rank
        height = fk * per_rank
        value = spread_k[at : at + height, :] * jnp.concatenate([root] * (height // 8), axis=0)
        k_out[at : at + height, :] = value.astype(bf16)


def call(kernel, name, out_shape, in_specs, scratch, flops, moved, out_specs=None, limit=8):
    return pl.pallas_call(
        kernel,
        name=name,
        out_shape=out_shape,
        in_specs=in_specs,
        out_specs=out_specs or jax.tree.map(lambda _: VMEM, out_shape),
        scratch_shapes=scratch,
        compiler_params=pltpu.CompilerParams(vmem_limit_bytes=limit * 2**20),
        cost_estimate=pl.CostEstimate(flops=flops, bytes_accessed=moved, transcendentals=0),
    )


def to_rows(array):
    slots, width = array.shape
    return array.reshape(slots, width // LANE, LANE).transpose(1, 0, 2).reshape(-1, LANE)


def from_rows(rows, slots):
    return rows.reshape(-1, slots, LANE).transpose(1, 0, 2).reshape(slots, -1)


def body(
    grad_query,
    grad_key,
    weight_query,
    weight_key,
    moment_query,
    moment_key,
    logit_peak,
    owner_table,
    head_order,
):
    owners = lax.axis_size("dp")
    ranks = lax.axis_size("mp")
    devices = owners * ranks
    layers, heads, piece_q = grad_query.shape
    piece_k = grad_key.shape[2]
    slots = moment_query.shape[0]
    per_rank = heads // ranks
    tiles = (piece_q + piece_k) // LANE
    kw = dict(ranks=ranks, owners=owners, slots=slots)
    shape = jax.ShapeDtypeStruct
    owner_2d = owner_table[:, :, 0].T
    head_row = head_order.reshape(1, heads)

    packed = call(
        functools.partial(pack_grads_kernel, **kw),
        "pack_grads",
        shape((devices * tiles * slots, LANE), bf16),
        [HBM] * 4,
        [
            pltpu.VMEM(owner_2d.shape, jnp.int32),
            pltpu.VMEM(head_row.shape, jnp.int32),
            pltpu.VMEM((layers * heads, piece_q), bf16),
            pltpu.VMEM((layers * heads, piece_k), bf16),
            pltpu.VMEM(((devices + 1) * tiles * slots, LANE), f32),
            pltpu.VMEM((devices * tiles * slots, LANE), bf16),
            pltpu.SemaphoreType.DMA((4,)),
            pltpu.SemaphoreType.DMA((4,)),
        ],
        2 * 256 * 128 * 2816,
        3 * 2**20,
        out_specs=HBM,
        limit=58,
    )(
        owner_2d,
        head_row,
        grad_query.reshape(layers * heads, piece_q),
        grad_key.reshape(layers * heads, piece_k),
    )
    packed = packed.reshape(devices, tiles, slots, LANE).transpose(0, 2, 1, 3).reshape(devices, slots, -1)
    owned = lax.all_to_all(packed, ("dp", "mp"), split_axis=0, concat_axis=0, tiled=True)
    owned = owned.reshape(devices, slots, tiles, LANE).transpose(0, 2, 1, 3).reshape(-1, LANE)

    wrows = layers * tiles * per_rank
    by_y = call(
        functools.partial(pack_weights_kernel, ranks=ranks),
        "pack_weights",
        [shape((SIDE, wrows, LANE), bf16)] * SIDE,
        [VMEM] * 3,
        [pltpu.VMEM(((ranks + 1) * wrows, LANE), f32)],
        2 * 128 * 64 * 2816,
        3 * 2**20,
    )(head_row, weight_query, weight_key)
    along_y = [
        [(i, i // SIDE * SIDE + (i + s) % SIDE) for i in range(ranks)] for s in range(SIDE)
    ]
    along_x = [[(i, (i + t * SIDE) % ranks) for i in range(ranks)] for t in range(SIDE)]
    peaks = logit_peak[0]
    for reach in (4, 1, 2):
        peaks = jnp.maximum(peaks, lax.ppermute(peaks, "dp", [(i, i ^ reach) for i in range(owners)]))
        if reach == 4:
            peaks, by_y = lax.optimization_barrier((peaks, by_y))
    by_y = [by_y[0]] + [lax.ppermute(by_y[s], "mp", along_y[s]) for s in range(1, SIDE)]
    fq = DQ * RQ // LANE
    fk = DN * RK // LANE
    parts = 4
    polar, next_q, next_k = call(
        functools.partial(polar_kernel, **kw),
        "polar",
        (
            shape((owners, slots * (fq + fk) // owners, LANE), bf16),
            shape((fq * slots, LANE), f32),
            shape((fk * slots, LANE), f32),
        ),
        [VMEM, VMEM, HBM, HBM],
        [
            pltpu.VMEM((fq * slots + RQ // LANE * slots, LANE), f32),
            pltpu.VMEM((fk * slots + RK // LANE * slots, LANE), f32),
            pltpu.VMEM((fq * slots, LANE), f32),
            pltpu.VMEM((fk * slots, LANE), f32),
            pltpu.VMEM((owners, slots * (fq + fk) // owners, LANE), bf16),
            pltpu.SemaphoreType.DMA((2 * parts,)),
            pltpu.SemaphoreType.DMA((2 * parts,)),
            pltpu.SemaphoreType.DMA,
        ],
        4 * 10**9,
        8 * 2**20,
        (HBM, HBM, HBM),
        50,
    )(owner_2d, owned, to_rows(moment_query), to_rows(moment_key))
    polar, by_y = lax.optimization_barrier((polar, by_y))
    by_x = [jnp.stack([block[t] for block in by_y], axis=0) for t in range(SIDE)]
    weights = [by_x[0]] + [lax.ppermute(by_x[t], "mp", along_x[t]) for t in range(1, SIDE)]
    back = lax.all_to_all(polar, "dp", split_axis=0, concat_axis=0, tiled=True)

    oq = layers * per_rank * fq // owners
    ok = layers * per_rank * fk // owners
    new_q, new_k = call(
        functools.partial(finish_kernel, **kw),
        "finish",
        (shape((oq, LANE), bf16), shape((ok, LANE), bf16)),
        [SMEM, SMEM, VMEM, VMEM] + [VMEM] * SIDE,
        [
            pltpu.VMEM((oq + RQ // LANE * per_rank, LANE), f32),
            pltpu.VMEM((ok + RK // LANE * per_rank, LANE), f32),
        ],
        10**7,
        4 * 2**20,
    )(owner_2d, head_order, peaks, back, *weights)

    def rollout(rows):
        rows = rows.reshape(layers, -1, per_rank, LANE).transpose(0, 2, 1, 3)
        return rows.reshape(layers, per_rank, -1)

    return rollout(new_q), rollout(new_k), from_rows(next_q, slots), from_rows(next_k, slots)


def solution(mesh):
    placed = (
        P(None, None, ("dp", "mp")),
        P(None, None, ("dp", "mp")),
        P(None, None, ("dp", "mp")),
        P(None, None, ("dp", "mp")),
        P(("dp", "mp"), None),
        P(("dp", "mp"), None),
        P("dp", None, None),
        P(),
        P(),
    )
    return jax.shard_map(
        body,
        mesh=mesh,
        in_specs=placed,
        out_specs=(
            P(None, "mp", "dp"),
            P(None, "mp", "dp"),
            P(("dp", "mp"), None),
            P(("dp", "mp"), None),
        ),
        check_vma=False,
    )
```
